128 devices in a mesh: gy: 16 (over x, z), gx: 8 (over y, core).
Axes of the slice: x: 4, y: 4, z: 4, core: 2. Of those that a mesh axis runs over, the one named last changes fastest.
Arguments:
- coarse: bfloat16 [256, 70, 128], P(('gy', 'gx')), may hold values from -6 to 6
- enc_weight: bfloat16 [70, 128], replicated, may hold values from -0.75 to 0.75
- enc_bias: float32 [128], replicated, may hold values from -3 to 3
- block_ids: int32 [128, 16], P(('gy', 'gx')), may hold values from 0 to 255, as said below
- interp_index: int32 [128, 16], P(('gy', 'gx')), may hold values from 0 to 3
- interp_table: bfloat16 [4, 8192, 128], replicated, may hold values from -0.125 to 0.125
- noise_index: int32 [1], replicated, may hold values from 0 to 63
- noise_table: float32 [64, 128], replicated, may hold values from -6 to 6
- fine: bfloat16 [1024, 1024, 128], P('gy', 'gx'), may hold values from -6 to 6
- conv_weight: bfloat16 [9, 128, 128], replicated, may hold values from -0.1875 to 0.1875
- cotangent: bfloat16 [1024, 1024, 128], P('gy', 'gx'), may hold values from -6 to 6
Outputs:
- output: bfloat16 [1024, 1024, 128], P('gy', 'gx')
- grad_fine: bfloat16 [1024, 1024, 128], P('gy', 'gx')
- grad_coarse: float32 [256, 70, 128], P(('gy', 'gx'))
- grad_enc_weight: float32 [70, 128], replicated
- grad_enc_bias: float32 [128], replicated
- grad_conv: float32 [9, 128, 128], replicated
The draws below stay inside these ranges and needn't reach their ends.
Inputs may be any that keep to these rules, and one draw needn't show every extreme that they name: `block_ids`: band b holds blocks b * 16 to (b + 1) * 16 - 1; the blocks named by a tile of fine tile row r lie in bands r - 1, r or r + 1.
All inputs are finite; a program needn't handle non-finite values.
Results may differ from the reference program's by a relative error of at most 0.0055.
Values may be sent and summed in bfloat16 or wider, within the bound.
No kernel may reach another device: no remote copies, remote signals or barrier semaphores. Data moves between devices by JAX's collectives and lax.ppermute only.
A program may use at most 192 MiB of HBM per device.

```python
import jax
import jax.numpy as jnp
from jax import lax

C = 128
V = 70
CB = 128
K = 16
NW = 4
NSIG = 64
TH = 64
TW = 128
ROWBLK = 16
BANDS = 16
TILES = 128
NBLK = 256
FH = 1024
FW = 1024
N_GY = 16
N_GX = 8


def draw_block_ids(key, part):
    key = jax.random.fold_in(key, 11)
    key_off, key_col, key_top, key_low = jax.random.split(key, 4)
    tile_row = jnp.arange(TILES, dtype=jnp.int32)[:, None] // (TILES // BANDS)
    offset = jax.random.randint(key_off, (TILES, K), -1, 2, dtype=jnp.int32)
    band = jnp.clip(tile_row + offset, 0, BANDS - 1)
    column = jax.random.randint(key_col, (TILES, K), 0, ROWBLK, dtype=jnp.int32)
    ids = band * ROWBLK + column
    slot_top = jax.random.randint(key_top, (), 0, K, dtype=jnp.int32)
    slot_low = jax.random.randint(key_low, (), 0, K, dtype=jnp.int32)
    ids = ids.at[TILES - 1, slot_top].set(NBLK - 1)
    ids = ids.at[0, slot_low].set(0)
    return ids.astype(jnp.int32)


def set_ends(array, own_key, least, high):
    longest = array.shape.index(max(array.shape))
    spots = []
    for shift in (0, 1):
        where = [jax.random.randint(jax.random.fold_in(own_key, axis), (), 0, length) for axis, length in enumerate(array.shape)]
        where[longest] = (where[longest] + shift) % array.shape[longest]
        spots.append(tuple(where))
    return array.at[spots[0]].set(least).at[spots[1]].set(high)


def block_levels(rng, extent, pieces, low, top_value):
    def one(dim, shards_of):
        draws = jax.random.uniform(jax.random.fold_in(jax.random.fold_in(rng, 6), dim), (shards_of,), jnp.float32, low / len(pieces), top_value / len(pieces))
        return jnp.repeat(jnp.exp(draws), extent[dim] // shards_of).reshape((-1,) + (1,) * (len(extent) - dim - 1))

    level = one(*pieces[0])
    for cut in pieces[1:]:
        level = level * one(*cut)
    return level


def noise(stream_key, shape, scale, bound, cuts=(), held_as=jnp.bfloat16):
    array = scale * jax.random.normal(stream_key, shape, jnp.float32)
    if cuts:
        array = array * block_levels(stream_key, shape, cuts, -0.22, 0.18)
    return jnp.clip(array, -bound, bound).astype(held_as)


def setup_inputs(seed: int = 0) -> dict:
    key_list = jax.random.split(jax.random.key(seed), 12)
    return {
        "coarse": noise(key_list[0], (NBLK, V, CB), 1.0, 6.0, ((0, 128),)),
        "enc_weight": noise(key_list[1], (V, C), V ** -0.5, 0.75),
        "enc_bias": noise(key_list[2], (C,), 0.5, 3.0, (), jnp.float32),
        "block_ids": draw_block_ids(jax.random.fold_in(key_list[11], 71), 0),
        "interp_index": set_ends(jax.random.randint(key_list[4], (TILES, K), 0, NW), jax.random.fold_in(key_list[4], 1), 0, NW - 1).astype(jnp.int32),
        "interp_table": noise(key_list[5], (NW, TH * TW, CB), (K * CB) ** -0.5, 0.125),
        "noise_index": jax.random.randint(key_list[6], (1,), 0, NSIG).astype(jnp.int32),
        "noise_table": noise(key_list[7], (NSIG, C), 1.0, 6.0, (), jnp.float32),
        "fine": noise(key_list[8], (FH, FW, C), 1.0, 6.0, ((0, 16), (1, 8))),
        "conv_weight": noise(key_list[9], (9, C, C), (9 * C) ** -0.5, 0.1875),
        "cotangent": noise(key_list[10], (FH, FW, C), 1.0, 6.0, ((0, 16), (1, 8))),
    }


def silu_grad(value):
    sig = jax.nn.sigmoid(value)
    return sig * (1.0 + value * (1.0 - sig))

def to_tiles(field):
    return field.reshape(N_GY, TH, N_GX, TW, field.shape[-1]).transpose(0, 2, 1, 3, 4).reshape(TILES, TH * TW, field.shape[-1])

def from_tiles(tiles):
    return tiles.reshape(N_GY, N_GX, TH, TW, tiles.shape[-1]).transpose(0, 2, 1, 3, 4).reshape(FH, FW, tiles.shape[-1])

def reference(coarse, enc_weight, enc_bias, block_ids, interp_index, interp_table, noise_index, noise_table, fine, conv_weight, cotangent):
    hp = lax.Precision.HIGHEST
    coarse_f = coarse.astype(jnp.float32)
    weight_f = enc_weight.astype(jnp.float32)
    pre = jnp.einsum('nvb,vc->nbc', coarse_f, weight_f, precision=hp) + enc_bias
    encoded = jax.nn.silu(pre).astype(jnp.bfloat16)

    def lift_tile(t):
        blocks = encoded[block_ids[t]].astype(jnp.float32)
        mats = interp_table[interp_index[t]].astype(jnp.float32)
        return jnp.einsum('kmb,kbc->mc', mats, blocks, precision=hp)
    lifted = from_tiles(lax.map(lift_tile, jnp.arange(TILES)))
    act = fine.astype(jnp.float32) + lifted + noise_table[noise_index[0]]
    smooth = jax.nn.silu(act).astype(jnp.bfloat16)
    padded = jnp.pad(smooth, ((1, 1), (1, 1), (0, 0)))
    conv = jnp.zeros((FH * FW, C), jnp.float32)
    for tap in range(9):
        dy, dx = (tap // 3, tap % 3)
        part = padded[dy:dy + FH, dx:dx + FW].reshape(FH * FW, C)
        conv = conv + jnp.dot(part, conv_weight[tap], preferred_element_type=jnp.float32)
    output = (act + conv.reshape(FH, FW, C)).astype(jnp.bfloat16)
    cot_pad = jnp.pad(cotangent, ((1, 1), (1, 1), (0, 0)))
    cot_flat = cotangent.reshape(FH * FW, C)
    back = jnp.zeros((FH * FW, C), jnp.float32)
    taps = []
    for tap in range(9):
        dy, dx = (tap // 3, tap % 3)
        part = cot_pad[2 - dy:2 - dy + FH, 2 - dx:2 - dx + FW].reshape(FH * FW, C)
        back = back + jnp.dot(part, conv_weight[tap].T, preferred_element_type=jnp.float32)
        near = padded[dy:dy + FH, dx:dx + FW].reshape(FH * FW, C)
        taps.append(jnp.dot(near.T, cot_flat, preferred_element_type=jnp.float32))
    grad_conv = jnp.stack(taps)
    grad_fine = (cotangent.astype(jnp.float32) + silu_grad(act) * back.reshape(FH, FW, C)).astype(jnp.bfloat16)
    grad_tiles = to_tiles(grad_fine)

    def tile_terms(t):
        mats = interp_table[interp_index[t]].astype(jnp.float32)
        return jnp.einsum('kmb,mc->kbc', mats, grad_tiles[t].astype(jnp.float32), precision=hp)
    terms = lax.map(tile_terms, jnp.arange(TILES))
    grad_encoded = jax.ops.segment_sum(terms.reshape(TILES * K, CB, C), block_ids.reshape(-1), NBLK)
    grad_pre = grad_encoded * silu_grad(pre)
    grad_coarse = jnp.einsum('vc,nbc->nvb', weight_f, grad_pre, precision=hp)
    grad_enc_weight = jnp.einsum('nvb,nbc->vc', coarse_f, grad_pre, precision=hp)
    grad_enc_bias = lax.optimization_barrier(jnp.sum(grad_pre, axis=(0, 1)))
    return (output, grad_fine, grad_coarse, grad_enc_weight, grad_enc_bias, grad_conv)
```

```python
import functools

import jax
import jax.numpy as jnp
from jax import lax
from jax.experimental import pallas as pl
from jax.experimental.pallas import tpu as pltpu
from jax.sharding import PartitionSpec as P

BF = jnp.bfloat16
F32 = jnp.float32
VP = 80
META = 16
CHUNK = 8
PACK = 16
VMEM = pl.BlockSpec(memory_space=pltpu.VMEM)
SMEM = pl.BlockSpec(memory_space=pltpu.SMEM)
HBM = pl.BlockSpec(memory_space=pl.ANY)


def mm(a, b):
    return jnp.dot(a, b, preferred_element_type=F32)


def mm_t(a, b):
    return lax.dot_general(a, b, (((1,), (1,)), ((), ())), preferred_element_type=F32)


def t_mm(a, b):
    return lax.dot_general(a, b, (((0,), (0,)), ((), ())), preferred_element_type=F32)


def sigmoid(v):
    return 0.5 * jnp.tanh(0.5 * v) + 0.5


def shifted_rows(x_ref, top_ref, bot_ref, left_ref, right_ref, pad_ref):
    def emit(row, r, parity, half):
        row = row.astype(F32)
        cell = lax.broadcasted_iota(jnp.int32, row.shape, 0)
        size = row.shape[0]
        low = jnp.where(cell == 0, left_ref[r], pltpu.roll(row, 1, 0))
        high = jnp.where(cell == size - 1, right_ref[r], pltpu.roll(row, size - 1, 0))
        pad_ref[0, parity, half] = low.astype(BF)
        pad_ref[1, parity, half] = row.astype(BF)
        pad_ref[2, parity, half] = high.astype(BF)

    pairs = x_ref.shape[0] // 2
    emit(top_ref[...], 0, 0, 0)
    emit(bot_ref[...], 2 * pairs + 1, 1, pairs)

    def step(m, _):
        emit(x_ref[2 * m], 2 * m + 1, 1, m)
        emit(x_ref[2 * m + 1], 2 * m + 2, 0, m + 1)
        return 0

    lax.fori_loop(0, pairs, step, 0, unroll=2)


def windows(pad_ref, start, count):
    cells, chans = pad_ref.shape[3:]
    return jnp.concatenate(
        [
            pad_ref[d, rho % 2, pl.ds(start + rho // 2, count)].reshape(count * cells, chans)
            for rho in range(4)
            for d in range(3)
        ],
        axis=1,
    )


def back_kernel(cot_ref, top_ref, bot_ref, left_ref, right_ref, w_ref, back_ref, pad_ref, taps_ref):
    cells, chans = cot_ref.shape[1:]
    taps_ref[...] = jnp.zeros_like(taps_ref)
    for dy in range(3):
        for dx in range(3):
            for o in range(2):
                col = ((o + 2 - dy) * 3 + 2 - dx) * chans
                taps_ref[o * chans : (o + 1) * chans, col : col + chans] = w_ref[3 * dy + dx]
    shifted_rows(cot_ref, top_ref, bot_ref, left_ref, right_ref, pad_ref)
    count = 4

    def step(c, _):
        acc = mm_t(windows(pad_ref, c * count, count), taps_ref[...]).astype(BF)
        for o in range(2):
            part = acc[:, o * chans : (o + 1) * chans].reshape(count, cells, chans)
            back_ref[pl.ds(c * count, count), o] = part
        return 0

    lax.fori_loop(0, back_ref.shape[0] // count, step, 0)


def conv_kernel(
    smooth_ref, top_ref, bot_ref, left_ref, right_ref, w_ref, act_ref, out_ref, pad_ref, taps_ref
):
    cells, chans = smooth_ref.shape[1:]
    taps_ref[...] = jnp.zeros_like(taps_ref)
    for dy in range(3):
        for dx in range(3):
            for o in range(2):
                row = ((o + dy) * 3 + dx) * chans
                taps_ref[row : row + chans, o * chans : (o + 1) * chans] = w_ref[3 * dy + dx]
    shifted_rows(smooth_ref, top_ref, bot_ref, left_ref, right_ref, pad_ref)
    count = 4

    def step(c, _):
        acc = mm(windows(pad_ref, c * count, count), taps_ref[...])
        for o in range(2):
            part = acc[:, o * chans : (o + 1) * chans].reshape(count, cells, chans)
            act = act_ref[pl.ds(c * count, count), o].astype(F32)
            out_ref[pl.ds(c * count, count), o] = (act + part).astype(BF)
        return 0

    lax.fori_loop(0, out_ref.shape[0] // count, step, 0)


def main_kernel(
    loc_ref,
    which_ref,
    noise_index_ref,
    noise_ref,
    window_ref,
    weight_ref,
    bias_row_ref,
    bias_col_ref,
    pad_hbm,
    fine_ref,
    cot_ref,
    back_ref,
    table_ref,
    smooth_ref,
    act_ref,
    gfine_ref,
    edges_ref,
    terms_ref,
    shared_ref,
    enc_ref,
    enc16_ref,
    terms_acc,
    flip_ref,
    pad_ref,
    sem,
):
    step = pl.program_id(0)
    steps = pl.num_programs(0)
    rows, cells, chans = fine_ref.shape
    slots = which_ref.shape[1]
    mats = table_ref.shape[0]
    rowblk = 16
    copy = pltpu.make_async_copy(pad_hbm, pad_ref, sem)

    def block(slot):
        at = loc_ref[0, slot]
        band = lax.div(at, rowblk)
        inner = lax.rem(at, rowblk)
        return window_ref[lax.div(inner, 2), band, lax.rem(inner, 2)]

    @pl.when(step == 0)
    def _():
        copy.start()
        enc_ref[...] = jnp.zeros_like(enc_ref)
        terms_acc[...] = jnp.zeros_like(terms_acc)
        for slot in range(slots):
            pre = t_mm(block(slot), weight_ref[...]) + bias_row_ref[...]
            encoded = (pre * sigmoid(pre)).astype(BF).astype(F32)
            enc_ref[which_ref[0, slot]] += encoded
        for w in range(mats):
            high = enc_ref[w].astype(BF)
            low = (enc_ref[w] - high.astype(F32)).astype(BF)
            enc16_ref[w * chans : (w + 1) * chans, :chans] = high
            enc16_ref[w * chans : (w + 1) * chans, chans:] = low

    table = jnp.concatenate([table_ref[w] for w in range(mats)], axis=1)
    both = mm(table, enc16_ref[...])
    lifted = both[:, :chans] + both[:, chans:]
    embed = noise_ref[pl.ds(noise_index_ref[0], 1), :]
    fine = fine_ref[...].reshape(rows * cells, chans).astype(F32)
    act = fine + lifted + embed
    sig = sigmoid(act)
    smooth = act * sig
    slope = sig * (1.0 + act * (1.0 - sig))
    cot = cot_ref[...].reshape(rows * cells, chans).astype(F32)
    back = back_ref[...].reshape(rows * cells, chans).astype(F32)
    gfine = (cot + slope * back).astype(BF)
    act_ref[...] = act.astype(BF).reshape(rows, cells, chans)
    gfine_ref[...] = gfine.reshape(rows, cells, chans)
    smooth3 = smooth.reshape(rows, cells, chans)
    smooth16 = smooth3.astype(BF)
    smooth_ref[...] = smooth16
    edges_ref[0] = smooth3[:, 0:1, :].astype(BF).astype(F32)
    edges_ref[1] = smooth3[:, cells - 1 : cells, :].astype(BF).astype(F32)
    for r in range(rows):
        at = pl.multiple_of((step * (rows // 2) + r // 2) * cells, cells)
        flip_ref[(r % 2) * chans : (r % 2 + 1) * chans, pl.ds(at, cells)] = smooth16[r].T
    terms_acc[...] += mm(gfine.T, table)

    @pl.when(step == steps - 1)
    def _():
        copy.wait()
        for w in range(mats):
            terms_ref[w] = terms_acc[:, w * chans : (w + 1) * chans].astype(BF)
        pairs = flip_ref.shape[1] // cells
        lhs = flip_ref[...]
        for d in range(3):
            found = {}
            for h in range(2):
                rhs = jnp.concatenate(
                    [pad_ref[d, q, h : h + pairs].reshape(pairs * cells, chans) for q in range(2)],
                    axis=1,
                )
                got = mm(lhs, rhs)
                for o in range(2):
                    for q in range(2):
                        found[o, 2 * h + q] = got[
                            o * chans : (o + 1) * chans, q * chans : (q + 1) * chans
                        ]
            for dy in range(3):
                tap = 3 * dy + 2 - d
                total = found[0, 2 - dy] + found[1, 3 - dy]
                shared_ref[tap * chans : (tap + 1) * chans, :] = total.astype(BF)
        base = 9 * chans
        vp = weight_ref.shape[0]

        def slot_grad(slot, totals):
            gweight, gbias = totals
            coarse = block(slot)
            pre = t_mm(weight_ref[...], coarse) + bias_col_ref[...]
            sig = sigmoid(pre)
            slope = sig * (1.0 + pre * (1.0 - sig))
            at = pl.multiple_of(which_ref[0, slot] * chans, chans)
            gpre = (terms_acc[:, pl.ds(at, chans)] * slope).astype(BF)
            ones = jnp.ones((16, chans), BF)
            return (gweight + mm_t(coarse, gpre), gbias + mm_t(ones, gpre))

        totals = (jnp.zeros((vp, chans), F32), jnp.zeros((16, chans), F32))
        gweight, gbias = lax.fori_loop(0, slots, slot_grad, totals, unroll=4)
        shared_ref[base : base + vp, :] = gweight.astype(BF)
        shared_ref[base + vp : base + vp + 16, :] = gbias.astype(BF)
        rest = shared_ref.shape[0] - base - vp - 16
        shared_ref[base + vp + 16 :, :] = jnp.zeros((rest, chans), BF)


def band_kernel(loc_ref, which_ref, above_ref, own_ref, below_ref, out_ref, acc_ref):
    acc_ref[...] = jnp.zeros_like(acc_ref)
    rowblk = acc_ref.shape[0]
    for tile, terms in enumerate((above_ref, own_ref, below_ref)):
        for slot in range(which_ref.shape[1]):
            at = loc_ref[tile, slot]

            @pl.when(jnp.logical_and(at >= 0, at < rowblk))
            def _():
                acc_ref[at] += terms[which_ref[tile, slot]].astype(F32)

    out_ref[...] = acc_ref[...].astype(BF)


def owner_kernel(got_ref, coarse_ref, weight_ref, bias_col_ref, out_ref):
    weight = weight_ref[...]
    for n in range(coarse_ref.shape[0]):
        total = got_ref[0, n].astype(F32)
        for source in range(1, got_ref.shape[0]):
            total = total + got_ref[source, n].astype(F32)
        pre = t_mm(weight, coarse_ref[n]) + bias_col_ref[...]
        sig = sigmoid(pre)
        gpre = total * (sig * (1.0 + pre * (1.0 - sig)))
        high = gpre.astype(BF)
        low = (gpre - high.astype(F32)).astype(BF)
        full = mm(weight, high) + mm(weight, low)
        out_ref[n] = full[: out_ref.shape[1], :]


def sum_kernel(got_ref, out_ref):
    total = jnp.sum(got_ref[...].astype(F32), axis=0).astype(BF)
    out_ref[...] = jnp.broadcast_to(total[None], out_ref.shape)


def params(mib):
    return pltpu.CompilerParams(vmem_limit_bytes=mib * 1024 * 1024)


def shape(dims, dtype=BF):
    return jax.ShapeDtypeStruct(dims, dtype)


def cost(flops, size):
    return pl.CostEstimate(flops=flops, bytes_accessed=size, transcendentals=0)


def body(
    coarse,
    enc_weight,
    enc_bias,
    block_ids,
    interp_index,
    interp_table,
    noise_index,
    noise_table,
    fine,
    conv_weight,
    cotangent,
):
    n_gy, n_gx = lax.axis_size("gy"), lax.axis_size("gx")
    per, variables, chans = coarse.shape
    rows, cells, _ = fine.shape
    rowblk = per * n_gx
    slots = block_ids.shape[1]
    down = [(i, i + 1) for i in range(n_gy - 1)]
    up = [(i + 1, i) for i in range(n_gy - 1)]
    right = [(i, i + 1) for i in range(n_gx - 1)]
    left = [(i + 1, i) for i in range(n_gx - 1)]
    gy = lax.axis_index("gy")

    coarse_pad = jnp.pad(coarse, ((0, 0), (0, VP - variables), (0, 0)))
    own = coarse_pad.reshape(per * VP, chans)
    weight_pad = jnp.pad(enc_weight, ((0, VP - variables), (0, 0)))
    bias_row = enc_bias.reshape(1, chans)
    bias_col = enc_bias.reshape(chans, 1)
    meta = jnp.concatenate([block_ids, interp_index], axis=1).astype(BF)
    meta = jnp.pad(meta, ((0, META - 1), (0, chans - 2 * slots)))

    from_above = lax.ppermute(jnp.concatenate([own, meta, cotangent[rows - 1]]), "gy", down)
    from_below = lax.ppermute(jnp.concatenate([own, meta, cotangent[0]]), "gy", up)
    nown = per * VP
    window = jnp.concatenate([from_above[:nown], own, from_below[:nown]])
    window = jnp.broadcast_to(window[None], (n_gx,) + window.shape)
    window = lax.all_to_all(window, "gx", 0, 0, tiled=True).reshape(n_gx, 3, per, VP, chans)
    above_meta = from_above[nown : nown + 1, : 2 * slots].astype(jnp.int32)
    below_meta = from_below[nown : nown + 1, : 2 * slots].astype(jnp.int32)
    loc_all = jnp.concatenate([above_meta[:, :slots], block_ids, below_meta[:, :slots]]) - gy * rowblk
    which_all = jnp.concatenate([above_meta[:, slots:], interp_index, below_meta[:, slots:]])

    cot_top, cot_bot = from_above[nown + META :], from_below[nown + META :]

    def columns(top, bot, first, last):
        to_left = jnp.concatenate([top[:1], first, bot[:1]])
        to_right = jnp.concatenate([top[cells - 1 :], last, bot[cells - 1 :]])
        from_left = lax.ppermute(to_right, "gx", right).astype(F32)
        from_right = lax.ppermute(to_left, "gx", left).astype(F32)
        return from_left.reshape(rows + 2, 1, chans), from_right.reshape(rows + 2, 1, chans)

    cot_left, cot_right = columns(cot_top, cot_bot, cotangent[:, 0], cotangent[:, cells - 1])

    pairs = rows // 2
    pad_shape = (3, 2, pairs + 1, cells, chans)
    field = (rows, cells, chans)
    conv_flops = 2 * pairs * cells * 12 * chans * 2 * chans
    back, cot_pad = pl.pallas_call(
        back_kernel,
        out_shape=(shape((pairs, 2, cells, chans)), shape(pad_shape)),
        in_specs=[VMEM] * 6,
        out_specs=(VMEM, VMEM),
        scratch_shapes=[pltpu.VMEM((2 * chans, 12 * chans), BF)],
        compiler_params=params(40),
        cost_estimate=cost(conv_flops, 12 << 20),
        name="back",
    )(cotangent, cot_top, cot_bot, cot_left, cot_right, conv_weight)

    steps = rows // CHUNK
    mats = interp_table.shape[0]
    table = interp_table
    rows_spec = pl.BlockSpec((CHUNK, cells, chans), lambda i: (i, 0, 0))
    n_dev = n_gy * n_gx
    smooth, act, grad_fine, edges, terms, shared = pl.pallas_call(
        main_kernel,
        grid=(steps,),
        out_shape=(
            shape(field),
            shape(field),
            shape(field),
            shape((2, rows, 1, chans), F32),
            shape((mats, chans, chans)),
            shape((n_dev * PACK, chans)),
        ),
        in_specs=[
            SMEM,
            SMEM,
            SMEM,
            VMEM,
            VMEM,
            VMEM,
            VMEM,
            VMEM,
            HBM,
            rows_spec,
            rows_spec,
            rows_spec,
            pl.BlockSpec((mats, CHUNK * cells, chans), lambda i: (0, i, 0)),
        ],
        out_specs=(
            rows_spec,
            rows_spec,
            rows_spec,
            pl.BlockSpec((2, CHUNK, 1, chans), lambda i: (0, i, 0, 0)),
            VMEM,
            VMEM,
        ),
        scratch_shapes=[
            pltpu.VMEM((mats, chans, chans), F32),
            pltpu.VMEM((mats * chans, 2 * chans), BF),
            pltpu.VMEM((chans, mats * chans), F32),
            pltpu.VMEM((2 * chans, pairs * cells), BF),
            pltpu.VMEM(pad_shape, BF),
            pltpu.SemaphoreType.DMA,
        ],
        compiler_params=params(48),
        cost_estimate=cost(3 * conv_flops, 24 << 20),
        name="main",
    )(
        loc_all[1:2] + rowblk,
        interp_index,
        noise_index,
        noise_table,
        window,
        weight_pad,
        bias_row,
        bias_col,
        cot_pad,
        fine,
        cotangent,
        back.reshape(field),
        table,
    )

    both = ("gy", "gx")
    parts = lax.all_to_all(shared.reshape(n_dev, PACK, chans), both, 0, 0, tiled=True)

    smooth_top = lax.ppermute(smooth[rows - 1], "gy", down)
    smooth_bot = lax.ppermute(smooth[0], "gy", up)
    terms_above = lax.ppermute(terms, "gy", down)
    terms_below = lax.ppermute(terms, "gy", up)
    band = pl.pallas_call(
        band_kernel,
        out_shape=shape((rowblk, chans, chans)),
        in_specs=[SMEM, SMEM, VMEM, VMEM, VMEM],
        out_specs=VMEM,
        scratch_shapes=[pltpu.VMEM((rowblk, chans, chans), F32)],
        compiler_params=params(16),
        cost_estimate=cost(1 << 22, 1 << 20),
        name="band",
    )(loc_all, which_all, terms_above, terms, terms_below)
    owned = lax.all_to_all(band.reshape(n_gx, per, chans, chans), "gx", 0, 0, tiled=True)
    edges = edges.astype(BF).reshape(2, rows, chans)
    smooth_left, smooth_right = columns(smooth_top, smooth_bot, edges[0], edges[1])
    output = pl.pallas_call(
        conv_kernel,
        out_shape=shape((pairs, 2, cells, chans)),
        in_specs=[VMEM] * 7,
        out_specs=VMEM,
        scratch_shapes=[
            pltpu.VMEM(pad_shape, BF),
            pltpu.VMEM((12 * chans, 2 * chans), BF),
        ],
        compiler_params=params(40),
        cost_estimate=cost(conv_flops, 8 << 20),
        name="conv",
    )(
        smooth,
        smooth_top,
        smooth_bot,
        smooth_left,
        smooth_right,
        conv_weight,
        act.reshape(pairs, 2, cells, chans),
    ).reshape(field)
    grad_coarse = pl.pallas_call(
        owner_kernel,
        out_shape=shape(coarse.shape, F32),
        in_specs=[VMEM] * 4,
        out_specs=VMEM,
        compiler_params=params(16),
        name="owner",
    )(owned, coarse_pad, weight_pad, bias_col)

    summed = pl.pallas_call(
        sum_kernel,
        out_shape=shape((n_dev, PACK, chans)),
        in_specs=[VMEM],
        out_specs=VMEM,
        compiler_params=params(16),
        name="total",
    )(parts)
    total = lax.all_to_all(summed, both, 0, 0, tiled=True).reshape(n_dev * PACK, chans).astype(F32)
    base = 9 * chans
    grad_conv = total[:base].reshape(9, chans, chans)
    grad_weight = total[base : base + variables]
    grad_bias = total[base + VP]
    return (output, grad_fine, grad_coarse, grad_weight, grad_bias, grad_conv)


def solution(mesh):
    placed = (
        P(("gy", "gx"), None, None),
        P(),
        P(),
        P(("gy", "gx"), None),
        P(("gy", "gx"), None),
        P(),
        P(),
        P(),
        P("gy", "gx", None),
        P(),
        P("gy", "gx", None),
    )
    return jax.shard_map(
        body,
        mesh=mesh,
        in_specs=placed,
        out_specs=(
            P("gy", "gx", None),
            P("gy", "gx", None),
            P(("gy", "gx"), None, None),
            P(),
            P(),
            P(),
        ),
        check_vma=False,
    )
```

```python
import functools

import jax
import jax.numpy as jnp
from jax import lax
from jax.experimental import pallas as pl
from jax.experimental.pallas import tpu as pltpu
from jax.sharding import PartitionSpec as P

BF = jnp.bfloat16
F32 = jnp.float32
VP = 80
META = 16
CHUNK = 16
PAIRS = 8
PACK = 16
LIMIT = 52
VMEM = pl.BlockSpec(memory_space=pltpu.VMEM)
SMEM = pl.BlockSpec(memory_space=pltpu.SMEM)
HBM = pl.BlockSpec(memory_space=pl.ANY)


def mm(a, b):
    return jnp.dot(a, b, preferred_element_type=F32)


def mm_t(a, b):
    return lax.dot_general(a, b, (((1,), (1,)), ((), ())), preferred_element_type=F32)


def t_mm(a, b):
    return lax.dot_general(a, b, (((0,), (0,)), ((), ())), preferred_element_type=F32)


def sigmoid(v):
    return 0.5 * jnp.tanh(0.5 * v) + 0.5


def put_row(row, r, at, half, left_ref, right_ref, pad_ref):
    row = row.astype(F32)
    size, chans = row.shape
    cell = lax.broadcasted_iota(jnp.int32, row.shape, 0)
    low = jnp.where(cell == 0, left_ref[pl.ds(r, 1), :], pltpu.roll(row, 1, 0))
    high = jnp.where(cell == size - 1, right_ref[pl.ds(r, 1), :], pltpu.roll(row, size - 1, 0))
    lanes = slice(half * chans, (half + 1) * chans)
    pad_ref[0, at, :, lanes] = low.astype(BF)
    pad_ref[1, at, :, lanes] = row.astype(BF)
    pad_ref[2, at, :, lanes] = high.astype(BF)


def place_columns(got_left, got_right, left_ref, right_ref):
    rows = got_left.shape[0] - 32
    left_ref[...] = got_left.astype(F32)
    right_ref[...] = got_right.astype(F32)
    for at in (rows, rows + 16):
        left_ref[at : at + 1, :] = left_ref[at + 15 : at + 16, :]


def put_pairs(x_ref, start, count, left_ref, right_ref, pad_ref):
    for k in range(count):
        m = start + k
        put_row(x_ref[2 * m], 2 * m, m, 1, left_ref, right_ref, pad_ref)
        put_row(x_ref[2 * m + 1], 2 * m + 1, m + 1, 0, left_ref, right_ref, pad_ref)


def windows(pad_ref, start, count):
    cells, lanes = pad_ref.shape[2:]
    return jnp.concatenate(
        [
            pad_ref[d, pl.ds(start + h, count)].reshape(count * cells, lanes)
            for h in range(2)
            for d in range(3)
        ],
        axis=1,
    )


def lane_of(rho, d):
    return ((rho // 2) * 3 + d) * 2 + rho % 2


def start_all(copies):
    for copy in copies:
        copy.start()


def wait_all(copies):
    for copy in copies:
        copy.wait()


def pack_kernel(
    coarse_ref, ids_hbm, which_hbm, cot_hbm, own_ref, all_ref, down_ref, up_ref,
    work_ref, meta_ref, small_ref, sems,
):
    per, variables, chans = coarse_ref.shape
    rows, cells = cot_hbm.shape[:2]
    copies = [
        pltpu.make_async_copy(ids_hbm, small_ref.at[0], sems.at[2]),
        pltpu.make_async_copy(which_hbm, small_ref.at[1], sems.at[3]),
        pltpu.make_async_copy(cot_hbm.at[rows - 1], down_ref.at[pl.ds(META, cells)], sems.at[0]),
        pltpu.make_async_copy(cot_hbm.at[0], up_ref.at[pl.ds(META, cells)], sems.at[1]),
    ]
    start_all(copies)
    work_ref[...] = jnp.zeros_like(work_ref)
    for n in range(per):
        work_ref[n * VP : n * VP + variables, :] = coarse_ref[n].astype(F32)
    work = work_ref[...].astype(BF)
    own_ref[...] = work
    for target in range(all_ref.shape[0]):
        all_ref[target] = work
    meta_ref[...] = jnp.zeros_like(meta_ref)
    wait_all(copies)
    slots = small_ref.shape[2]
    meta_ref[0:1, :slots] = small_ref[0].astype(F32)
    meta_ref[1:2, :slots] = small_ref[1].astype(F32)
    down_ref[:META, :] = meta_ref[...].astype(BF)
    up_ref[:META, :] = meta_ref[...].astype(BF)


def fill_columns(got_left, got_right, above_ref, below_ref, left_ref, right_ref, pad_ref):
    cells = pad_ref.shape[2]
    rows = got_left.shape[0] - 32
    place_columns(got_left, got_right, left_ref, right_ref)
    base = above_ref.shape[0] - cells
    put_row(above_ref[base:, :], rows + 16, 0, 0, left_ref, right_ref, pad_ref)
    put_row(below_ref[base:, :], rows, rows // 2, 1, left_ref, right_ref, pad_ref)


def back_kernel(
    cot_hbm, above_ref, below_ref, left16_ref, right16_ref, w_ref,
    back_hbm, cot_ref, back_ref, pad_ref, taps_ref, left_ref, right_ref, in_sems, out_sems,
):
    pairs, _, cells, chans = back_ref.shape
    count = PAIRS
    groups = pairs // count

    def fetch(g):
        at = pl.ds(g * 2 * count, 2 * count)
        return pltpu.make_async_copy(cot_hbm.at[at], cot_ref.at[at], in_sems.at[g])

    def send(g):
        at = pl.ds(g * count, count)
        return pltpu.make_async_copy(back_ref.at[at], back_hbm.at[at], out_sems.at[g])

    start_all([fetch(g) for g in range(groups)])
    taps_ref[...] = jnp.zeros_like(taps_ref)
    for dy in range(3):
        for dx in range(3):
            for o in range(2):
                col = lane_of(o + 2 - dy, 2 - dx) * chans
                taps_ref[o * chans : (o + 1) * chans, col : col + chans] = w_ref[3 * dy + dx]
    fill_columns(
        left16_ref[...], right16_ref[...], above_ref, below_ref, left_ref, right_ref, pad_ref
    )

    def pad(g, _):
        fetch(g).wait()
        put_pairs(cot_ref, g * count, count, left_ref, right_ref, pad_ref)
        return 0

    lax.fori_loop(0, groups, pad, 0)

    def step(g, _):
        acc = mm_t(windows(pad_ref, g * count, count), taps_ref[...]).astype(BF)
        for o in range(2):
            part = acc[:, o * chans : (o + 1) * chans].reshape(count, cells, chans)
            back_ref[pl.ds(g * count, count), o] = part
        send(g).start()
        return 0

    lax.fori_loop(0, groups, step, 0)
    wait_all([send(g) for g in range(groups)])


def conv_kernel(
    pos_ref, smooth_hbm, above_ref, below_ref, got_left_ref, got_right_ref, w_ref, act_hbm,
    out_hbm, smooth_ref, act_ref, out_ref, pad_ref, taps_ref, left_ref, right_ref, sems,
):
    pairs, _, cells, chans = out_ref.shape
    rows = 2 * pairs
    count = PAIRS
    groups = pairs // count

    def piece(src, dst, kind, g, size):
        at = pl.ds(g * size, size)
        return pltpu.make_async_copy(src.at[at], dst.at[at], sems.at[kind, g])

    def fetch(g):
        return piece(smooth_hbm, smooth_ref, 0, g, 2 * count)

    def fetch_act(g):
        return piece(act_hbm, act_ref, 1, g, count)

    def send(g):
        return piece(out_ref, out_hbm, 2, g, count)

    start_all([fetch(g) for g in range(groups)])
    start_all([fetch_act(g) for g in range(groups)])
    taps_ref[...] = jnp.zeros_like(taps_ref)
    for dy in range(3):
        for dx in range(3):
            for o in range(2):
                row = lane_of(o + dy, dx) * chans
                taps_ref[row : row + chans, o * chans : (o + 1) * chans] = w_ref[3 * dy + dx]
    gx, n_gx = pos_ref[1], pos_ref[2]
    base = got_left_ref.shape[0] - rows - 32
    from_left = jnp.where(gx > 0, got_left_ref[base:, :].astype(F32), 0.0)
    from_right = jnp.where(gx < n_gx - 1, got_right_ref[base:, :].astype(F32), 0.0)
    fill_columns(from_left, from_right, above_ref, below_ref, left_ref, right_ref, pad_ref)

    def pad(g, _):
        fetch(g).wait()
        put_pairs(smooth_ref, g * count, count, left_ref, right_ref, pad_ref)
        return 0

    lax.fori_loop(0, groups, pad, 0)

    def step(g, _):
        fetch_act(g).wait()
        acc = mm(windows(pad_ref, g * count, count), taps_ref[...])
        for o in range(2):
            part = acc[:, o * chans : (o + 1) * chans].reshape(count, cells, chans)
            act = act_ref[pl.ds(g * count, count), o].astype(F32)
            out_ref[pl.ds(g * count, count), o] = (act + part).astype(BF)
        send(g).start()
        return 0

    lax.fori_loop(0, groups, step, 0)
    wait_all([send(g) for g in range(groups)])


def main_kernel(
    pos_ref, ids_ref, which_ref, noise_index_ref, noise_ref, band_above_ref, band_own_ref, band_below_ref, weight_ref,
    bias_col_ref, above_ref, below_ref, left16_ref, right16_ref,
    fine_hbm, cot_hbm, back_hbm, table_hbm,
    smooth_hbm, act_hbm, gfine_hbm, edges_ref, terms_ref, down_ref, up_ref, shared_ref,
    pad_ref, cot_ref, fine_ref, back_ref, table_ref, smooth_ref, act_ref, gfine_ref,
    coarse_ref, slope_ref, gpre_ref, enc_ref, enc16_ref, terms_acc, flip_ref,
    left_ref, right_ref, in_sems, out_sems,
):
    total_rows, cells, chans = fine_ref.shape
    slots = which_ref.shape[1]
    mats = table_ref.shape[0]
    rows = CHUNK
    steps = total_rows // rows
    pairs = total_rows // 2
    rowblk = band_own_ref.shape[0] // VP
    first_band = pos_ref[0] * rowblk - rowblk

    def fetches(step):
        at = pl.ds(step * rows, rows)
        flat = pl.ds(step * rows * cells, rows * cells)
        return [
            pltpu.make_async_copy(table_hbm.at[:, flat], table_ref.at[:, flat], in_sems.at[0, step]),
            pltpu.make_async_copy(fine_hbm.at[at], fine_ref.at[at], in_sems.at[1, step]),
            pltpu.make_async_copy(back_hbm.at[at], back_ref.at[at], in_sems.at[2, step]),
            pltpu.make_async_copy(cot_hbm.at[at], cot_ref.at[at], in_sems.at[3, step]),
        ]

    def sends(step):
        at = pl.ds(step * rows, rows)
        return [
            pltpu.make_async_copy(smooth_ref.at[at], smooth_hbm.at[at], out_sems.at[0, step]),
            pltpu.make_async_copy(act_ref.at[at], act_hbm.at[at], out_sems.at[1, step]),
            pltpu.make_async_copy(gfine_ref.at[at], gfine_hbm.at[at], out_sems.at[2, step]),
        ]

    for step in range(steps):
        start_all(fetches(step))
    enc_ref[...] = jnp.zeros_like(enc_ref)
    terms_acc[...] = jnp.zeros_like(terms_acc)
    group = 4

    def encode(first, _):
        for k in range(group):
            slot = first * group + k
            at = ids_ref[0, slot] - first_band
            band = lax.div(at, rowblk)
            source = pl.ds(pl.multiple_of(lax.rem(at, rowblk) * VP, VP), VP)
            block = jnp.where(
                band == 1,
                band_own_ref[source, :],
                jnp.where(band == 0, band_above_ref[source, :], band_below_ref[source, :]),
            )
            coarse_ref[:, pl.ds(pl.multiple_of(slot * cells, cells), cells)] = block
        size = group * cells
        lanes = pl.ds(pl.multiple_of(first * size, size), size)
        pre = t_mm(weight_ref[...], coarse_ref[:, lanes]) + bias_col_ref[...]
        sig = sigmoid(pre)
        encoded = (pre * sig).astype(BF).astype(F32)
        slope_ref[:, lanes] = sig * (1.0 + pre * (1.0 - sig))
        for k in range(group):
            enc_ref[which_ref[0, first * group + k]] += encoded[:, k * cells : (k + 1) * cells]
        return 0

    lax.fori_loop(0, slots // group, encode, 0)
    for w in range(mats):
        high = enc_ref[w].astype(BF)
        low = (enc_ref[w] - high.astype(F32)).astype(BF)
        enc16_ref[:chans, w * cells : (w + 1) * cells] = high
        enc16_ref[chans:, w * cells : (w + 1) * cells] = low
    embed = noise_ref[pl.ds(noise_index_ref[0], 1), :]
    fill_columns(
        left16_ref[...], right16_ref[...], above_ref, below_ref, left_ref, right_ref, pad_ref
    )

    def chunk(step, _):
        wait_all(fetches(step))
        at = pl.ds(step * rows, rows)
        flat = pl.ds(pl.multiple_of(step * rows * cells, rows * cells), rows * cells)
        table = jnp.concatenate([table_ref[w, flat, :] for w in range(mats)], axis=1)
        both = mm_t(table, enc16_ref[...])
        lifted = both[:, :chans] + both[:, chans:]
        fine = fine_ref[at].reshape(rows * cells, chans).astype(F32)
        act = fine + lifted + embed
        sig = sigmoid(act)
        smooth = act * sig
        slope = sig * (1.0 + act * (1.0 - sig))
        cot = cot_ref[at].reshape(rows * cells, chans).astype(F32)
        back = back_ref[at].reshape(rows * cells, chans).astype(F32)
        gfine = (cot + slope * back).astype(BF)
        act_ref[at] = act.astype(BF).reshape(rows, cells, chans)
        gfine_ref[at] = gfine.reshape(rows, cells, chans)
        smooth3 = smooth.reshape(rows, cells, chans)
        smooth16 = smooth3.astype(BF)
        smooth_ref[at] = smooth16
        for r in range(rows):
            row = pl.ds(step * rows + r, 1)
            edges_ref[0, row, :] = smooth3[r, 0:1, :]
            edges_ref[1, row, :] = smooth3[r, cells - 1 : cells, :]
            lanes = pl.ds(pl.multiple_of((step * (rows // 2) + r // 2) * cells, cells), cells)
            flip_ref[(r % 2) * chans : (r % 2 + 1) * chans, lanes] = smooth16[r].T
        put_pairs(cot_ref, step * (rows // 2), rows // 2, left_ref, right_ref, pad_ref)
        terms_acc[...] += mm(gfine.T, table)
        start_all(sends(step))
        return 0

    lax.fori_loop(0, steps, chunk, 0)

    size = mats * chans
    for w in range(mats):
        terms = terms_acc[:, w * cells : (w + 1) * cells]
        terms_ref[w] = terms
        down_ref[w * chans : (w + 1) * chans, :] = terms.astype(BF)
        up_ref[w * chans : (w + 1) * chans, :] = terms.astype(BF)
    down_ref[size:, :] = smooth_ref[total_rows - 1]
    up_ref[size:, :] = smooth_ref[0]

    def conv_grad(d, _):
        found = []
        for h in range(2):
            rhs = pad_ref[d, h : h + pairs].reshape(pairs * cells, 2 * chans)
            found.append(mm(flip_ref[...], rhs))
        for dy in range(3):
            total = jnp.zeros((chans, chans), F32)
            for o in range(2):
                rho = o + 2 - dy
                lanes = slice(rho % 2 * chans, (rho % 2 + 1) * chans)
                total = total + found[rho // 2][o * chans : (o + 1) * chans, lanes]
            tap = pl.multiple_of((3 * dy + 2 - d) * chans, chans)
            shared_ref[pl.ds(tap, chans), :] = total.astype(BF)
        return 0

    lax.fori_loop(0, 3, conv_grad, 0)

    def slot_grad(slot, gsum):
        lanes = pl.ds(pl.multiple_of(slot * cells, cells), cells)
        gpre = terms_ref[which_ref[0, slot]] * slope_ref[:, lanes]
        gpre_ref[:, lanes] = gpre.astype(BF)
        return gsum + gpre

    gsum = lax.fori_loop(0, slots, slot_grad, jnp.zeros((chans, cells), F32), unroll=2)
    gweight = mm_t(coarse_ref[...], gpre_ref[...])
    ones = jnp.ones((16, cells), BF)
    high = gsum.astype(BF)
    gbias = mm_t(ones, high) + mm_t(ones, (gsum - high.astype(F32)).astype(BF))
    base = 9 * chans
    for part in (gweight, gbias):
        count = part.shape[0]
        high = part.astype(BF)
        shared_ref[base : base + count, :] = high
        shared_ref[base + count : base + 2 * count, :] = (part - high.astype(F32)).astype(BF)
        base += 2 * count
    shared_ref[base:, :] = jnp.zeros((shared_ref.shape[0] - base, chans), BF)
    for step in range(steps):
        wait_all(sends(step))


def band_kernel(
    pos_ref, loc_ref, which_ref, above_ref, own_ref, below_ref, edges_ref,
    mine_ref, *refs,
):
    outs, acc_ref = refs[:-1], refs[-1]
    acc_ref[...] = jnp.zeros_like(acc_ref)
    rowblk, chans, cells = acc_ref.shape

    def slot_terms(slot, _):
        for tile in range(3):
            at, w = loc_ref[tile, slot], which_ref[tile, slot]

            @pl.when(jnp.logical_and(at >= 0, at < rowblk))
            def _():
                if tile == 1:
                    acc_ref[at] += own_ref[w]
                else:
                    terms = (above_ref, below_ref)[tile // 2]
                    rows = pl.ds(pl.multiple_of(w * chans, chans), chans)
                    acc_ref[at] += terms[rows, :].astype(F32)

        return 0

    lax.fori_loop(0, which_ref.shape[1], slot_terms, 0)
    gx, n_gx = pos_ref[1], len(outs) + 1
    per = rowblk // n_gx
    for n in range(per):
        mine_ref[n] = acc_ref[gx * per + n]
    for k, out_ref in enumerate(outs, 1):
        target = lax.rem(gx + k, n_gx)
        for n in range(per):
            out_ref[n * chans : (n + 1) * chans, :] = acc_ref[target * per + n].astype(BF)
    if not outs:
        return
    size = above_ref.shape[0] - cells
    base = per * chans
    edge = edges_ref.shape[1]
    for out_ref, column, first in ((outs[0], 1, cells - 16), (outs[-1], 0, 0)):
        rows = slice(first, first + 16)
        out_ref[base : base + edge, :] = edges_ref[column].astype(BF)
        out_ref[base + edge : base + edge + 16, :] = below_ref[size:, :][rows]
        out_ref[base + edge + 16 :, :] = above_ref[size:, :][rows]


def owner_kernel(mine_ref, coarse_ref, weight_ref, bias_col_ref, *refs):
    gots, out_ref = refs[:-1], refs[-1]
    weight = weight_ref[...]
    chans = weight.shape[1]
    for n in range(out_ref.shape[0]):
        total = mine_ref[n]
        for got_ref in gots:
            total = total + got_ref[n * chans : (n + 1) * chans, :].astype(F32)
        pre = t_mm(weight, coarse_ref[n * VP : (n + 1) * VP, :]) + bias_col_ref[...]
        sig = sigmoid(pre)
        gpre = total * (sig * (1.0 + pre * (1.0 - sig)))
        high = gpre.astype(BF)
        low = (gpre - high.astype(F32)).astype(BF)
        full = mm(weight, high) + mm(weight, low)
        out_ref[n] = full[: out_ref.shape[1], :]


def sum_kernel(got_ref, out_ref):
    total = jnp.sum(got_ref[...].astype(F32), axis=0).astype(BF)
    out_ref[...] = jnp.broadcast_to(total[None], out_ref.shape)


def finish_kernel(got_ref, gconv_ref, gweight_ref, gbias_ref):
    taps, chans, _ = gconv_ref.shape
    variables = gweight_ref.shape[0]
    for tap in range(taps):
        gconv_ref[tap] = got_ref[tap * chans : (tap + 1) * chans, :].astype(F32)
    base = taps * chans
    high = got_ref[base : base + VP, :].astype(F32)
    low = got_ref[base + VP : base + 2 * VP, :].astype(F32)
    gweight_ref[...] = (high + low)[:variables, :]
    base += 2 * VP
    high = got_ref[base : base + 16, :].astype(F32)
    low = got_ref[base + 16 : base + 32, :].astype(F32)
    gbias_ref[...] = (high + low)[:1, :]


def params(mib):
    return pltpu.CompilerParams(vmem_limit_bytes=mib * 1024 * 1024)


def shape(dims, dtype=BF):
    return jax.ShapeDtypeStruct(dims, dtype)


def cost(flops, size):
    return pl.CostEstimate(flops=flops, bytes_accessed=size, transcendentals=0)


def body(
    coarse,
    enc_weight,
    enc_bias,
    block_ids,
    interp_index,
    interp_table,
    noise_index,
    noise_table,
    fine,
    conv_weight,
    cotangent,
):
    n_gy, n_gx = lax.axis_size("gy"), lax.axis_size("gx")
    per, variables, chans = coarse.shape
    rows, cells, _ = fine.shape
    rowblk = per * n_gx
    slots = block_ids.shape[1]
    mats = interp_table.shape[0]
    pairs = rows // 2
    down = [(i, i + 1) for i in range(n_gy - 1)]
    up = [(i + 1, i) for i in range(n_gy - 1)]
    right = [(i, i + 1) for i in range(n_gx - 1)]
    left = [(i + 1, i) for i in range(n_gx - 1)]
    both = ("gy", "gx")
    gy = lax.axis_index("gy")
    pos = jnp.stack([gy, lax.axis_index("gx"), jnp.int32(n_gx)]).astype(jnp.int32)
    nown = per * VP

    own, spread, to_below, to_above = pl.pallas_call(
        pack_kernel,
        out_shape=(
            shape((nown, chans)),
            shape((n_gx, nown, chans)),
            shape((META + cells, chans)),
            shape((META + cells, chans)),
        ),
        in_specs=[VMEM, HBM, HBM, HBM],
        out_specs=(VMEM,) * 4,
        scratch_shapes=[
            pltpu.VMEM((nown, chans), F32),
            pltpu.VMEM((META, chans), F32),
            pltpu.VMEM((2, 1, slots), jnp.int32),
            pltpu.SemaphoreType.DMA((4,)),
        ],
        compiler_params=params(LIMIT),
        name="pack",
    )(coarse, block_ids, interp_index, cotangent)
    band_own = lax.all_to_all(spread, "gx", 0, 0, tiled=True).reshape(rowblk * VP, chans)
    from_above = lax.ppermute(to_below, "gy", down)
    from_below = lax.ppermute(to_above, "gy", up)
    to_left = jnp.concatenate(
        [cotangent[:, 0], from_below[META : META + 16], from_above[META : META + 16]]
    )
    to_right = jnp.concatenate(
        [
            cotangent[:, cells - 1],
            from_below[META + cells - 16 :],
            from_above[META + cells - 16 :],
        ]
    )
    cot_left = lax.ppermute(to_right, "gx", right)
    cot_right = lax.ppermute(to_left, "gx", left)
    band_above = lax.ppermute(band_own, "gy", down)
    band_below = lax.ppermute(band_own, "gy", up)

    weight_pad = jnp.pad(enc_weight, ((0, VP - variables), (0, 0)))
    bias_col = enc_bias.reshape(chans, 1)
    pad_shape = (3, pairs + 1, cells, 2 * chans)
    field = (rows, cells, chans)
    paired = (pairs, 2, cells, chans)
    columns = pltpu.VMEM((rows + 32, chans), F32)
    conv_flops = 2 * pairs * cells * 12 * chans * 2 * chans
    groups = pairs // PAIRS
    back = pl.pallas_call(
        back_kernel,
        out_shape=shape(paired),
        in_specs=[HBM] + [VMEM] * 5,
        out_specs=HBM,
        scratch_shapes=[
            pltpu.VMEM(field, BF),
            pltpu.VMEM(paired, BF),
            pltpu.VMEM(pad_shape, BF),
            pltpu.VMEM((2 * chans, 12 * chans), BF),
            columns,
            columns,
            pltpu.SemaphoreType.DMA((groups,)),
            pltpu.SemaphoreType.DMA((groups,)),
        ],
        compiler_params=params(LIMIT),
        cost_estimate=cost(conv_flops, 12 << 20),
        name="back",
    )(cotangent, from_above, from_below, cot_left, cot_right, conv_weight)

    n_dev = n_gy * n_gx
    steps = rows // CHUNK
    smooth, act, grad_fine, edges, terms, to_below, to_above, shared = pl.pallas_call(
        main_kernel,
        out_shape=(
            shape(field),
            shape(field),
            shape(field),
            shape((2, rows, chans), F32),
            shape((mats, chans, chans), F32),
            shape((mats * chans + cells, chans)),
            shape((mats * chans + cells, chans)),
            shape((n_dev * PACK, chans)),
        ),
        in_specs=[SMEM] * 4 + [VMEM] * 10 + [HBM] * 4,
        out_specs=(HBM,) * 3 + (VMEM,) * 5,
        scratch_shapes=[
            pltpu.VMEM(pad_shape, BF),
            pltpu.VMEM(field, BF),
            pltpu.VMEM(field, BF),
            pltpu.VMEM(field, BF),
            pltpu.VMEM(interp_table.shape, BF),
            pltpu.VMEM(field, BF),
            pltpu.VMEM(field, BF),
            pltpu.VMEM(field, BF),
            pltpu.VMEM((VP, slots * chans), BF),
            pltpu.VMEM((chans, slots * chans), F32),
            pltpu.VMEM((chans, slots * chans), BF),
            pltpu.VMEM((mats, chans, chans), F32),
            pltpu.VMEM((2 * chans, mats * chans), BF),
            pltpu.VMEM((chans, mats * chans), F32),
            pltpu.VMEM((2 * chans, pairs * cells), BF),
            columns,
            columns,
            pltpu.SemaphoreType.DMA((4, steps)),
            pltpu.SemaphoreType.DMA((3, steps)),
        ],
        compiler_params=params(LIMIT),
        cost_estimate=cost(3 * conv_flops, 24 << 20),
        name="main",
    )(
        pos,
        block_ids,
        interp_index,
        noise_index,
        noise_table,
        band_above,
        band_own,
        band_below,
        weight_pad,
        bias_col,
        from_above,
        from_below,
        cot_left,
        cot_right,
        fine,
        cotangent,
        back.reshape(field),
        interp_table,
    )

    parts = lax.all_to_all(shared.reshape(n_dev, PACK, chans), both, 0, 0, tiled=True)

    below2 = lax.ppermute(to_above, "gy", up)
    above2 = lax.ppermute(to_below, "gy", down)
    above_meta = from_above[:2, :slots].astype(jnp.int32)
    below_meta = from_below[:2, :slots].astype(jnp.int32)
    loc_all = jnp.concatenate([above_meta[:1], block_ids, below_meta[:1]]) - gy * rowblk
    which_all = jnp.concatenate([above_meta[1:], interp_index, below_meta[1:]])
    plain, full = per * chans, per * chans + rows + 32
    lengths = [full if k in (1, n_gx - 1) else plain for k in range(1, n_gx)]
    mine, *sent = pl.pallas_call(
        band_kernel,
        out_shape=[shape((per, chans, chans), F32)] + [shape((n, chans)) for n in lengths],
        in_specs=[SMEM] * 3 + [VMEM] * 4,
        out_specs=[VMEM] * n_gx,
        scratch_shapes=[pltpu.VMEM((rowblk, chans, chans), F32)],
        compiler_params=params(8),
        cost_estimate=cost(1 << 22, 1 << 20),
        name="band",
    )(pos, loc_all, which_all, above2, terms, below2, edges)
    got = [
        lax.ppermute(part, "gx", [(i, (i + k) % n_gx) for i in range(n_gx)])
        for k, part in enumerate(sent, 1)
    ]

    summed = pl.pallas_call(
        sum_kernel,
        out_shape=shape((n_dev, PACK, chans)),
        in_specs=[VMEM],
        out_specs=VMEM,
        compiler_params=params(8),
        name="total",
    )(parts)
    total = lax.all_to_all(summed, both, 0, 0, tiled=True).reshape(n_dev * PACK, chans)

    output = pl.pallas_call(
        conv_kernel,
        out_shape=shape(paired),
        in_specs=[SMEM, HBM] + [VMEM] * 5 + [HBM],
        out_specs=HBM,
        scratch_shapes=[
            pltpu.VMEM(field, BF),
            pltpu.VMEM(paired, BF),
            pltpu.VMEM(paired, BF),
            pltpu.VMEM(pad_shape, BF),
            pltpu.VMEM((12 * chans, 2 * chans), BF),
            columns,
            columns,
            pltpu.SemaphoreType.DMA((3, groups)),
        ],
        compiler_params=params(LIMIT),
        cost_estimate=cost(conv_flops, 8 << 20),
        name="conv",
    )(pos, smooth, above2, below2, got[0], got[-1], conv_weight, act.reshape(paired))
    output, mine = lax.optimization_barrier((output, mine))
    grad_coarse = pl.pallas_call(
        owner_kernel,
        out_shape=shape(coarse.shape, F32),
        in_specs=[VMEM] * (3 + n_gx),
        out_specs=VMEM,
        compiler_params=params(8),
        name="owner",
    )(mine, own, weight_pad, bias_col, *got)
    grad_conv, grad_weight, grad_bias = pl.pallas_call(
        finish_kernel,
        out_shape=(
            shape((9, chans, chans), F32),
            shape((variables, chans), F32),
            shape((1, chans), F32),
        ),
        in_specs=[VMEM],
        out_specs=(VMEM,) * 3,
        compiler_params=params(8),
        name="finish",
    )(total)
    return (
        output.reshape(field),
        grad_fine,
        grad_coarse,
        grad_weight,
        grad_bias.reshape(chans),
        grad_conv,
    )


def solution(mesh):
    placed = (
        P(("gy", "gx"), None, None),
        P(),
        P(),
        P(("gy", "gx"), None),
        P(("gy", "gx"), None),
        P(),
        P(),
        P(),
        P("gy", "gx", None),
        P(),
        P("gy", "gx", None),
    )
    return jax.shard_map(
        body,
        mesh=mesh,
        in_specs=placed,
        out_specs=(
            P("gy", "gx", None),
            P("gy", "gx", None),
            P(("gy", "gx"), None, None),
            P(),
            P(),
            P(),
        ),
        check_vma=False,
    )
```

```python
import functools

import jax
import jax.numpy as jnp
from jax import lax
from jax.experimental import pallas as pl
from jax.experimental.pallas import tpu as pltpu
from jax.sharding import PartitionSpec as P

BF = jnp.bfloat16
F32 = jnp.float32
VP = 80
META = 16
CHUNK = 16
PAIRS = 8
PACK = 16
LIMIT = 52
VMEM = pl.BlockSpec(memory_space=pltpu.VMEM)
SMEM = pl.BlockSpec(memory_space=pltpu.SMEM)
HBM = pl.BlockSpec(memory_space=pl.ANY)


def mm(a, b):
    return jnp.dot(a, b, preferred_element_type=F32)


def mm_t(a, b):
    return lax.dot_general(a, b, (((1,), (1,)), ((), ())), preferred_element_type=F32)


def t_mm(a, b):
    return lax.dot_general(a, b, (((0,), (0,)), ((), ())), preferred_element_type=F32)


def sigmoid(v):
    return 0.5 * jnp.tanh(0.5 * v) + 0.5


def put_row(row, r, at, half, left_ref, right_ref, pad_ref):
    row = row.astype(F32)
    size, chans = row.shape
    cell = lax.broadcasted_iota(jnp.int32, row.shape, 0)
    low = jnp.where(cell == 0, left_ref[pl.ds(r, 1), :], pltpu.roll(row, 1, 0))
    high = jnp.where(cell == size - 1, right_ref[pl.ds(r, 1), :], pltpu.roll(row, size - 1, 0))
    lanes = slice(half * chans, (half + 1) * chans)
    pad_ref[0, at, :, lanes] = low.astype(BF)
    pad_ref[1, at, :, lanes] = row.astype(BF)
    pad_ref[2, at, :, lanes] = high.astype(BF)


def place_columns(got_left, got_right, left_ref, right_ref):
    rows = got_left.shape[0] - 32
    left_ref[...] = got_left.astype(F32)
    right_ref[...] = got_right.astype(F32)
    for at in (rows, rows + 16):
        left_ref[at : at + 1, :] = left_ref[at + 15 : at + 16, :]


def put_pairs(x_ref, start, count, left_ref, right_ref, pad_ref):
    for k in range(count):
        m = start + k
        put_row(x_ref[2 * m], 2 * m, m, 1, left_ref, right_ref, pad_ref)
        put_row(x_ref[2 * m + 1], 2 * m + 1, m + 1, 0, left_ref, right_ref, pad_ref)


def windows(pad_ref, start, count):
    cells, lanes = pad_ref.shape[2:]
    return jnp.concatenate(
        [
            pad_ref[d, pl.ds(start + h, count)].reshape(count * cells, lanes)
            for h in range(2)
            for d in range(3)
        ],
        axis=1,
    )


def lane_of(rho, d):
    return ((rho // 2) * 3 + d) * 2 + rho % 2


def start_all(copies):
    for copy in copies:
        copy.start()


def wait_all(copies):
    for copy in copies:
        copy.wait()


def pack_kernel(
    coarse_ref, ids_hbm, which_hbm, cot_hbm, own_ref, all_ref, down_ref, up_ref,
    work_ref, meta_ref, small_ref, sems,
):
    per, variables, chans = coarse_ref.shape
    rows, cells = cot_hbm.shape[:2]
    copies = [
        pltpu.make_async_copy(ids_hbm, small_ref.at[0], sems.at[2]),
        pltpu.make_async_copy(which_hbm, small_ref.at[1], sems.at[3]),
        pltpu.make_async_copy(cot_hbm.at[rows - 1], down_ref.at[pl.ds(META, cells)], sems.at[0]),
        pltpu.make_async_copy(cot_hbm.at[0], up_ref.at[pl.ds(META, cells)], sems.at[1]),
    ]
    start_all(copies)
    work_ref[...] = jnp.zeros_like(work_ref)
    for n in range(per):
        work_ref[n * VP : n * VP + variables, :] = coarse_ref[n].astype(F32)
    work = work_ref[...].astype(BF)
    own_ref[...] = work
    for target in range(all_ref.shape[0]):
        all_ref[target] = work
    meta_ref[...] = jnp.zeros_like(meta_ref)
    wait_all(copies)
    slots = small_ref.shape[2]
    meta_ref[0:1, :slots] = small_ref[0].astype(F32)
    meta_ref[1:2, :slots] = small_ref[1].astype(F32)
    down_ref[:META, :] = meta_ref[...].astype(BF)
    up_ref[:META, :] = meta_ref[...].astype(BF)


def fill_columns(got_left, got_right, above_ref, below_ref, left_ref, right_ref, pad_ref):
    cells = pad_ref.shape[2]
    rows = got_left.shape[0] - 32
    place_columns(got_left, got_right, left_ref, right_ref)
    base = above_ref.shape[0] - cells
    put_row(above_ref[base:, :], rows + 16, 0, 0, left_ref, right_ref, pad_ref)
    put_row(below_ref[base:, :], rows, rows // 2, 1, left_ref, right_ref, pad_ref)


def back_kernel(
    cot_hbm, above_ref, below_ref, left16_ref, right16_ref, w_ref,
    back_hbm, cot_ref, back_ref, pad_ref, taps_ref, left_ref, right_ref, in_sems, out_sems,
):
    pairs, _, cells, chans = back_ref.shape
    count = PAIRS
    groups = pairs // count

    def fetch(g):
        at = pl.ds(g * 2 * count, 2 * count)
        return pltpu.make_async_copy(cot_hbm.at[at], cot_ref.at[at], in_sems.at[g])

    def send(g):
        at = pl.ds(g * count, count)
        return pltpu.make_async_copy(back_ref.at[at], back_hbm.at[at], out_sems.at[g])

    start_all([fetch(g) for g in range(groups)])
    taps_ref[...] = jnp.zeros_like(taps_ref)
    for dy in range(3):
        for dx in range(3):
            for o in range(2):
                col = lane_of(o + 2 - dy, 2 - dx) * chans
                taps_ref[o * chans : (o + 1) * chans, col : col + chans] = w_ref[3 * dy + dx]
    fill_columns(
        left16_ref[...], right16_ref[...], above_ref, below_ref, left_ref, right_ref, pad_ref
    )

    def pad(g, _):
        fetch(g).wait()
        put_pairs(cot_ref, g * count, count, left_ref, right_ref, pad_ref)
        return 0

    lax.fori_loop(0, groups, pad, 0)

    def step(g, _):
        acc = mm_t(windows(pad_ref, g * count, count), taps_ref[...]).astype(BF)
        for o in range(2):
            part = acc[:, o * chans : (o + 1) * chans].reshape(count, cells, chans)
            back_ref[pl.ds(g * count, count), o] = part
        send(g).start()
        return 0

    lax.fori_loop(0, groups, step, 0)
    wait_all([send(g) for g in range(groups)])


def conv_kernel(
    pos_ref, smooth_hbm, above_ref, below_ref, got_left_ref, got_right_ref, w_ref, act_hbm,
    out_hbm, smooth_ref, act_ref, out_ref, pad_ref, taps_ref, left_ref, right_ref, sems,
):
    pairs, _, cells, chans = out_ref.shape
    rows = 2 * pairs
    count = PAIRS
    groups = pairs // count

    def piece(src, dst, kind, g, size):
        at = pl.ds(g * size, size)
        return pltpu.make_async_copy(src.at[at], dst.at[at], sems.at[kind, g])

    def fetch(g):
        return piece(smooth_hbm, smooth_ref, 0, g, 2 * count)

    def fetch_act(g):
        return piece(act_hbm, act_ref, 1, g, count)

    def send(g):
        return piece(out_ref, out_hbm, 2, g, count)

    start_all([fetch(g) for g in range(groups)])
    start_all([fetch_act(g) for g in range(groups)])
    taps_ref[...] = jnp.zeros_like(taps_ref)
    for dy in range(3):
        for dx in range(3):
            for o in range(2):
                row = lane_of(o + dy, dx) * chans
                taps_ref[row : row + chans, o * chans : (o + 1) * chans] = w_ref[3 * dy + dx]
    gx, n_gx = pos_ref[1], pos_ref[2]
    base = got_left_ref.shape[0] - rows - 32
    from_left = jnp.where(gx > 0, got_left_ref[base:, :].astype(F32), 0.0)
    from_right = jnp.where(gx < n_gx - 1, got_right_ref[base:, :].astype(F32), 0.0)
    fill_columns(from_left, from_right, above_ref, below_ref, left_ref, right_ref, pad_ref)

    def pad(g, _):
        fetch(g).wait()
        put_pairs(smooth_ref, g * count, count, left_ref, right_ref, pad_ref)
        return 0

    lax.fori_loop(0, groups, pad, 0)

    def step(g, _):
        fetch_act(g).wait()
        acc = mm(windows(pad_ref, g * count, count), taps_ref[...])
        for o in range(2):
            part = acc[:, o * chans : (o + 1) * chans].reshape(count, cells, chans)
            act = act_ref[pl.ds(g * count, count), o].astype(F32)
            out_ref[pl.ds(g * count, count), o] = (act + part).astype(BF)
        send(g).start()
        return 0

    lax.fori_loop(0, groups, step, 0)
    wait_all([send(g) for g in range(groups)])


def main_kernel(
    pos_ref, ids_ref, which_ref, noise_index_ref, noise_ref, band_above_ref, band_own_ref, band_below_ref, weight_ref,
    bias_col_ref, above_ref, below_ref, left16_ref, right16_ref,
    fine_hbm, cot_hbm, back_hbm, table_hbm,
    smooth_hbm, act_hbm, gfine_hbm, edges_ref, terms_ref, down_ref, up_ref, shared_ref,
    pad_ref, cot_ref, fine_ref, back_ref, table_ref, smooth_ref, act_ref, gfine_ref,
    coarse_ref, slope_ref, gpre_ref, enc_ref, enc16_ref, terms_acc, flip_ref,
    left_ref, right_ref, in_sems, out_sems,
):
    total_rows, cells, chans = fine_ref.shape
    slots = which_ref.shape[1]
    mats = table_ref.shape[0]
    rows = CHUNK
    steps = total_rows // rows
    pairs = total_rows // 2
    rowblk = band_own_ref.shape[0] // VP
    first_band = pos_ref[0] * rowblk - rowblk

    def fetches(step):
        at = pl.ds(step * rows, rows)
        flat = pl.ds(step * rows * cells, rows * cells)
        return [
            pltpu.make_async_copy(table_hbm.at[:, flat], table_ref.at[:, flat], in_sems.at[0, step]),
            pltpu.make_async_copy(fine_hbm.at[at], fine_ref.at[at], in_sems.at[1, step]),
            pltpu.make_async_copy(back_hbm.at[at], back_ref.at[at], in_sems.at[2, step]),
            pltpu.make_async_copy(cot_hbm.at[at], cot_ref.at[at], in_sems.at[3, step]),
        ]

    def sends(step):
        at = pl.ds(step * rows, rows)
        return [
            pltpu.make_async_copy(smooth_ref.at[at], smooth_hbm.at[at], out_sems.at[0, step]),
            pltpu.make_async_copy(act_ref.at[at], act_hbm.at[at], out_sems.at[1, step]),
            pltpu.make_async_copy(gfine_ref.at[at], gfine_hbm.at[at], out_sems.at[2, step]),
        ]

    for step in range(steps):
        start_all(fetches(step))
    enc_ref[...] = jnp.zeros_like(enc_ref)
    terms_acc[...] = jnp.zeros_like(terms_acc)
    group = 4

    def encode(first, _):
        for k in range(group):
            slot = first * group + k
            at = ids_ref[0, slot] - first_band
            band = lax.div(at, rowblk)
            source = pl.ds(pl.multiple_of(lax.rem(at, rowblk) * VP, VP), VP)
            block = jnp.where(
                band == 1,
                band_own_ref[source, :],
                jnp.where(band == 0, band_above_ref[source, :], band_below_ref[source, :]),
            )
            coarse_ref[:, pl.ds(pl.multiple_of(slot * cells, cells), cells)] = block
        size = group * cells
        lanes = pl.ds(pl.multiple_of(first * size, size), size)
        pre = t_mm(weight_ref[...], coarse_ref[:, lanes]) + bias_col_ref[...]
        sig = sigmoid(pre)
        encoded = (pre * sig).astype(BF).astype(F32)
        slope_ref[:, lanes] = sig * (1.0 + pre * (1.0 - sig))
        for k in range(group):
            enc_ref[which_ref[0, first * group + k]] += encoded[:, k * cells : (k + 1) * cells]
        return 0

    lax.fori_loop(0, slots // group, encode, 0)
    for w in range(mats):
        enc16_ref[:, w * cells : (w + 1) * cells] = enc_ref[w].astype(BF)
    embed = noise_ref[pl.ds(noise_index_ref[0], 1), :]
    fill_columns(
        left16_ref[...], right16_ref[...], above_ref, below_ref, left_ref, right_ref, pad_ref
    )

    def chunk(step, _):
        wait_all(fetches(step))
        at = pl.ds(step * rows, rows)
        flat = pl.ds(pl.multiple_of(step * rows * cells, rows * cells), rows * cells)
        table = jnp.concatenate([table_ref[w, flat, :] for w in range(mats)], axis=1)
        lifted = mm_t(table, enc16_ref[...])
        fine = fine_ref[at].reshape(rows * cells, chans).astype(F32)
        act = fine + lifted + embed
        sig = sigmoid(act)
        smooth = act * sig
        slope = sig * (1.0 + act * (1.0 - sig))
        cot = cot_ref[at].reshape(rows * cells, chans).astype(F32)
        back = back_ref[at].reshape(rows * cells, chans).astype(F32)
        gfine = (cot + slope * back).astype(BF)
        act_ref[at] = act.astype(BF).reshape(rows, cells, chans)
        gfine_ref[at] = gfine.reshape(rows, cells, chans)
        smooth3 = smooth.reshape(rows, cells, chans)
        smooth16 = smooth3.astype(BF)
        smooth_ref[at] = smooth16
        for r in range(rows):
            row = pl.ds(step * rows + r, 1)
            edges_ref[0, row, :] = smooth3[r, 0:1, :]
            edges_ref[1, row, :] = smooth3[r, cells - 1 : cells, :]
            lanes = pl.ds(pl.multiple_of((step * (rows // 2) + r // 2) * cells, cells), cells)
            flip_ref[(r % 2) * chans : (r % 2 + 1) * chans, lanes] = smooth16[r].T
        put_pairs(cot_ref, step * (rows // 2), rows // 2, left_ref, right_ref, pad_ref)
        terms_acc[...] += mm(gfine.T, table)
        return 0

    lax.fori_loop(0, steps, chunk, 0)
    for step in range(steps):
        start_all(sends(step))

    size = mats * chans
    for w in range(mats):
        terms = terms_acc[:, w * cells : (w + 1) * cells]
        terms_ref[w] = terms
        down_ref[w * chans : (w + 1) * chans, :] = terms.astype(BF)
        up_ref[w * chans : (w + 1) * chans, :] = terms.astype(BF)
    down_ref[size:, :] = smooth_ref[total_rows - 1]
    up_ref[size:, :] = smooth_ref[0]

    def conv_grad(d):
        found = []
        for h in range(2):
            rhs = pad_ref[d, h : h + pairs].reshape(pairs * cells, 2 * chans)
            found.append(mm(flip_ref[...], rhs))
        for dy in range(3):
            total = jnp.zeros((chans, chans), F32)
            for o in range(2):
                rho = o + 2 - dy
                lanes = slice(rho % 2 * chans, (rho % 2 + 1) * chans)
                total = total + found[rho // 2][o * chans : (o + 1) * chans, lanes]
            tap = (3 * dy + 2 - d) * chans
            shared_ref[pl.ds(tap, chans), :] = total.astype(BF)

    for d in range(3):
        conv_grad(d)

    def slot_grad(slot, gsum):
        lanes = pl.ds(pl.multiple_of(slot * cells, cells), cells)
        gpre = terms_ref[which_ref[0, slot]] * slope_ref[:, lanes]
        gpre_ref[:, lanes] = gpre.astype(BF)
        return gsum + gpre

    gsum = lax.fori_loop(0, slots, slot_grad, jnp.zeros((chans, cells), F32), unroll=2)
    gweight = mm_t(coarse_ref[...], gpre_ref[...])
    ones = jnp.ones((16, cells), BF)
    high = gsum.astype(BF)
    gbias = mm_t(ones, high) + mm_t(ones, (gsum - high.astype(F32)).astype(BF))
    base = 9 * chans
    for part in (gweight, gbias):
        count = part.shape[0]
        high = part.astype(BF)
        shared_ref[base : base + count, :] = high
        shared_ref[base + count : base + 2 * count, :] = (part - high.astype(F32)).astype(BF)
        base += 2 * count
    shared_ref[base:, :] = jnp.zeros((shared_ref.shape[0] - base, chans), BF)
    for step in range(steps):
        wait_all(sends(step))


def band_kernel(
    pos_ref, loc_ref, which_ref, above_ref, own_ref, below_ref, edges_ref,
    mine_ref, *refs,
):
    outs, acc_ref = refs[:-1], refs[-1]
    acc_ref[...] = jnp.zeros_like(acc_ref)
    rowblk, chans, cells = acc_ref.shape

    def slot_terms(slot, _):
        for tile in range(3):
            at, w = loc_ref[tile, slot], which_ref[tile, slot]

            @pl.when(jnp.logical_and(at >= 0, at < rowblk))
            def _():
                if tile == 1:
                    acc_ref[at] += own_ref[w]
                else:
                    terms = (above_ref, below_ref)[tile // 2]
                    rows = pl.ds(pl.multiple_of(w * chans, chans), chans)
                    acc_ref[at] += terms[rows, :].astype(F32)

        return 0

    lax.fori_loop(0, which_ref.shape[1], slot_terms, 0)
    gx, n_gx = pos_ref[1], len(outs) + 1
    per = rowblk // n_gx
    for n in range(per):
        mine_ref[n] = acc_ref[gx * per + n]
    for k, out_ref in enumerate(outs, 1):
        target = lax.rem(gx + k, n_gx)
        for n in range(per):
            out_ref[n * chans : (n + 1) * chans, :] = acc_ref[target * per + n].astype(BF)
    if not outs:
        return
    size = above_ref.shape[0] - cells
    base = per * chans
    edge = edges_ref.shape[1]
    for out_ref, column, first in ((outs[0], 1, cells - 16), (outs[-1], 0, 0)):
        rows = slice(first, first + 16)
        out_ref[base : base + edge, :] = edges_ref[column].astype(BF)
        out_ref[base + edge : base + edge + 16, :] = below_ref[size:, :][rows]
        out_ref[base + edge + 16 :, :] = above_ref[size:, :][rows]


def owner_kernel(mine_ref, coarse_ref, weight_ref, bias_col_ref, *refs):
    gots, out_ref = refs[:-1], refs[-1]
    weight = weight_ref[...]
    chans = weight.shape[1]
    for n in range(out_ref.shape[0]):
        total = mine_ref[n]
        for got_ref in gots:
            total = total + got_ref[n * chans : (n + 1) * chans, :].astype(F32)
        pre = t_mm(weight, coarse_ref[n * VP : (n + 1) * VP, :]) + bias_col_ref[...]
        sig = sigmoid(pre)
        gpre = total * (sig * (1.0 + pre * (1.0 - sig)))
        high = gpre.astype(BF)
        low = (gpre - high.astype(F32)).astype(BF)
        full = mm(weight, high) + mm(weight, low)
        out_ref[n] = full[: out_ref.shape[1], :]


def sum_kernel(got_ref, out_ref):
    total = jnp.sum(got_ref[...].astype(F32), axis=0).astype(BF)
    out_ref[...] = jnp.broadcast_to(total[None], out_ref.shape)


def finish_kernel(got_ref, gconv_ref, gweight_ref, gbias_ref):
    taps, chans, _ = gconv_ref.shape
    variables = gweight_ref.shape[0]
    for tap in range(taps):
        gconv_ref[tap] = got_ref[tap * chans : (tap + 1) * chans, :].astype(F32)
    base = taps * chans
    high = got_ref[base : base + VP, :].astype(F32)
    low = got_ref[base + VP : base + 2 * VP, :].astype(F32)
    gweight_ref[...] = (high + low)[:variables, :]
    base += 2 * VP
    high = got_ref[base : base + 16, :].astype(F32)
    low = got_ref[base + 16 : base + 32, :].astype(F32)
    gbias_ref[...] = (high + low)[:1, :]


def params(mib):
    return pltpu.CompilerParams(vmem_limit_bytes=mib * 1024 * 1024)


def shape(dims, dtype=BF):
    return jax.ShapeDtypeStruct(dims, dtype)


def cost(flops, size):
    return pl.CostEstimate(flops=flops, bytes_accessed=size, transcendentals=0)


def body(
    coarse,
    enc_weight,
    enc_bias,
    block_ids,
    interp_index,
    interp_table,
    noise_index,
    noise_table,
    fine,
    conv_weight,
    cotangent,
):
    n_gy, n_gx = lax.axis_size("gy"), lax.axis_size("gx")
    per, variables, chans = coarse.shape
    rows, cells, _ = fine.shape
    rowblk = per * n_gx
    slots = block_ids.shape[1]
    mats = interp_table.shape[0]
    pairs = rows // 2
    down = [(i, i + 1) for i in range(n_gy - 1)]
    up = [(i + 1, i) for i in range(n_gy - 1)]
    right = [(i, i + 1) for i in range(n_gx - 1)]
    left = [(i + 1, i) for i in range(n_gx - 1)]
    both = ("gy", "gx")
    gy = lax.axis_index("gy")
    pos = jnp.stack([gy, lax.axis_index("gx"), jnp.int32(n_gx)]).astype(jnp.int32)
    nown = per * VP

    own, spread, to_below, to_above = pl.pallas_call(
        pack_kernel,
        out_shape=(
            shape((nown, chans)),
            shape((n_gx, nown, chans)),
            shape((META + cells, chans)),
            shape((META + cells, chans)),
        ),
        in_specs=[VMEM, HBM, HBM, HBM],
        out_specs=(VMEM,) * 4,
        scratch_shapes=[
            pltpu.VMEM((nown, chans), F32),
            pltpu.VMEM((META, chans), F32),
            pltpu.VMEM((2, 1, slots), jnp.int32),
            pltpu.SemaphoreType.DMA((4,)),
        ],
        compiler_params=params(LIMIT),
        name="pack",
    )(coarse, block_ids, interp_index, cotangent)
    band_own = lax.all_to_all(spread, "gx", 0, 0, tiled=True).reshape(rowblk * VP, chans)
    from_above = lax.ppermute(to_below, "gy", down)
    from_below = lax.ppermute(to_above, "gy", up)
    to_left = jnp.concatenate(
        [cotangent[:, 0], from_below[META : META + 16], from_above[META : META + 16]]
    )
    to_right = jnp.concatenate(
        [
            cotangent[:, cells - 1],
            from_below[META + cells - 16 :],
            from_above[META + cells - 16 :],
        ]
    )
    cot_left = lax.ppermute(to_right, "gx", right)
    cot_right = lax.ppermute(to_left, "gx", left)
    band_above = lax.ppermute(band_own, "gy", down)
    band_below = lax.ppermute(band_own, "gy", up)

    weight_pad = jnp.pad(enc_weight, ((0, VP - variables), (0, 0)))
    bias_col = enc_bias.reshape(chans, 1)
    pad_shape = (3, pairs + 1, cells, 2 * chans)
    field = (rows, cells, chans)
    paired = (pairs, 2, cells, chans)
    columns = pltpu.VMEM((rows + 32, chans), F32)
    conv_flops = 2 * pairs * cells * 12 * chans * 2 * chans
    groups = pairs // PAIRS
    back = pl.pallas_call(
        back_kernel,
        out_shape=shape(paired),
        in_specs=[HBM] + [VMEM] * 5,
        out_specs=HBM,
        scratch_shapes=[
            pltpu.VMEM(field, BF),
            pltpu.VMEM(paired, BF),
            pltpu.VMEM(pad_shape, BF),
            pltpu.VMEM((2 * chans, 12 * chans), BF),
            columns,
            columns,
            pltpu.SemaphoreType.DMA((groups,)),
            pltpu.SemaphoreType.DMA((groups,)),
        ],
        compiler_params=params(LIMIT),
        cost_estimate=cost(conv_flops, 12 << 20),
        name="back",
    )(cotangent, from_above, from_below, cot_left, cot_right, conv_weight)

    n_dev = n_gy * n_gx
    steps = rows // CHUNK
    smooth, act, grad_fine, edges, terms, to_below, to_above, shared = pl.pallas_call(
        main_kernel,
        out_shape=(
            shape(field),
            shape(field),
            shape(field),
            shape((2, rows, chans), F32),
            shape((mats, chans, chans), F32),
            shape((mats * chans + cells, chans)),
            shape((mats * chans + cells, chans)),
            shape((n_dev * PACK, chans)),
        ),
        in_specs=[SMEM] * 4 + [VMEM] * 10 + [HBM] * 4,
        out_specs=(HBM,) * 3 + (VMEM,) * 5,
        scratch_shapes=[
            pltpu.VMEM(pad_shape, BF),
            pltpu.VMEM(field, BF),
            pltpu.VMEM(field, BF),
            pltpu.VMEM(field, BF),
            pltpu.VMEM(interp_table.shape, BF),
            pltpu.VMEM(field, BF),
            pltpu.VMEM(field, BF),
            pltpu.VMEM(field, BF),
            pltpu.VMEM((VP, slots * chans), BF),
            pltpu.VMEM((chans, slots * chans), F32),
            pltpu.VMEM((chans, slots * chans), BF),
            pltpu.VMEM((mats, chans, chans), F32),
            pltpu.VMEM((chans, mats * chans), BF),
            pltpu.VMEM((chans, mats * chans), F32),
            pltpu.VMEM((2 * chans, pairs * cells), BF),
            columns,
            columns,
            pltpu.SemaphoreType.DMA((4, steps)),
            pltpu.SemaphoreType.DMA((3, steps)),
        ],
        compiler_params=params(LIMIT),
        cost_estimate=cost(3 * conv_flops, 24 << 20),
        name="main",
    )(
        pos,
        block_ids,
        interp_index,
        noise_index,
        noise_table,
        band_above,
        band_own,
        band_below,
        weight_pad,
        bias_col,
        from_above,
        from_below,
        cot_left,
        cot_right,
        fine,
        cotangent,
        back.reshape(field),
        interp_table,
    )

    parts = lax.all_to_all(shared.reshape(n_dev, PACK, chans), both, 0, 0, tiled=True)

    below2 = lax.ppermute(to_above, "gy", up)
    above2 = lax.ppermute(to_below, "gy", down)
    above_meta = from_above[:2, :slots].astype(jnp.int32)
    below_meta = from_below[:2, :slots].astype(jnp.int32)
    loc_all = jnp.concatenate([above_meta[:1], block_ids, below_meta[:1]]) - gy * rowblk
    which_all = jnp.concatenate([above_meta[1:], interp_index, below_meta[1:]])
    plain, full = per * chans, per * chans + rows + 32
    lengths = [full if k in (1, n_gx - 1) else plain for k in range(1, n_gx)]
    mine, *sent = pl.pallas_call(
        band_kernel,
        out_shape=[shape((per, chans, chans), F32)] + [shape((n, chans)) for n in lengths],
        in_specs=[SMEM] * 3 + [VMEM] * 4,
        out_specs=[VMEM] * n_gx,
        scratch_shapes=[pltpu.VMEM((rowblk, chans, chans), F32)],
        compiler_params=params(8),
        cost_estimate=cost(1 << 22, 1 << 20),
        name="band",
    )(pos, loc_all, which_all, above2, terms, below2, edges)
    got = [
        lax.ppermute(part, "gx", [(i, (i + k) % n_gx) for i in range(n_gx)])
        for k, part in enumerate(sent, 1)
    ]

    summed = pl.pallas_call(
        sum_kernel,
        out_shape=shape((n_dev, PACK, chans)),
        in_specs=[VMEM],
        out_specs=VMEM,
        compiler_params=params(8),
        name="total",
    )(parts)
    total = lax.all_to_all(summed, both, 0, 0, tiled=True).reshape(n_dev * PACK, chans)

    output = pl.pallas_call(
        conv_kernel,
        out_shape=shape(paired),
        in_specs=[SMEM, HBM] + [VMEM] * 5 + [HBM],
        out_specs=HBM,
        scratch_shapes=[
            pltpu.VMEM(field, BF),
            pltpu.VMEM(paired, BF),
            pltpu.VMEM(paired, BF),
            pltpu.VMEM(pad_shape, BF),
            pltpu.VMEM((12 * chans, 2 * chans), BF),
            columns,
            columns,
            pltpu.SemaphoreType.DMA((3, groups)),
        ],
        compiler_params=params(LIMIT),
        cost_estimate=cost(conv_flops, 8 << 20),
        name="conv",
    )(pos, smooth, above2, below2, got[0], got[-1], conv_weight, act.reshape(paired))
    output, mine = lax.optimization_barrier((output, mine))
    grad_coarse = pl.pallas_call(
        owner_kernel,
        out_shape=shape(coarse.shape, F32),
        in_specs=[VMEM] * (3 + n_gx),
        out_specs=VMEM,
        compiler_params=params(8),
        name="owner",
    )(mine, own, weight_pad, bias_col, *got)
    grad_conv, grad_weight, grad_bias = pl.pallas_call(
        finish_kernel,
        out_shape=(
            shape((9, chans, chans), F32),
            shape((variables, chans), F32),
            shape((1, chans), F32),
        ),
        in_specs=[VMEM],
        out_specs=(VMEM,) * 3,
        compiler_params=params(8),
        name="finish",
    )(total)
    return (
        output.reshape(field),
        grad_fine,
        grad_coarse,
        grad_weight,
        grad_bias.reshape(chans),
        grad_conv,
    )


def solution(mesh):
    placed = (
        P(("gy", "gx"), None, None),
        P(),
        P(),
        P(("gy", "gx"), None),
        P(("gy", "gx"), None),
        P(),
        P(),
        P(),
        P("gy", "gx", None),
        P(),
        P("gy", "gx", None),
    )
    return jax.shard_map(
        body,
        mesh=mesh,
        in_specs=placed,
        out_specs=(
            P("gy", "gx", None),
            P("gy", "gx", None),
            P(("gy", "gx"), None, None),
            P(),
            P(),
            P(),
        ),
        check_vma=False,
    )
```

```python
import functools

import jax
import jax.numpy as jnp
from jax import lax
from jax.experimental import pallas as pl
from jax.experimental.pallas import tpu as pltpu
from jax.sharding import PartitionSpec as P

BF = jnp.bfloat16
F32 = jnp.float32
VP = 80
META = 16
CHUNK = 16
PAIRS = 8
PACK = 16
LIMIT = 52
VMEM = pl.BlockSpec(memory_space=pltpu.VMEM)
SMEM = pl.BlockSpec(memory_space=pltpu.SMEM)
HBM = pl.BlockSpec(memory_space=pl.ANY)


def mm(a, b):
    return jnp.dot(a, b, preferred_element_type=F32)


def mm_t(a, b):
    return lax.dot_general(a, b, (((1,), (1,)), ((), ())), preferred_element_type=F32)


def t_mm(a, b):
    return lax.dot_general(a, b, (((0,), (0,)), ((), ())), preferred_element_type=F32)


def sigmoid(v):
    return 0.5 * jnp.tanh(0.5 * v) + 0.5


def put_row(row, r, at, half, left_ref, right_ref, pad_ref):
    row = row.astype(F32)
    size, chans = row.shape
    cell = lax.broadcasted_iota(jnp.int32, row.shape, 0)
    low = jnp.where(cell == 0, left_ref[pl.ds(r, 1), :], pltpu.roll(row, 1, 0))
    high = jnp.where(cell == size - 1, right_ref[pl.ds(r, 1), :], pltpu.roll(row, size - 1, 0))
    lanes = slice(half * chans, (half + 1) * chans)
    pad_ref[0, at, :, lanes] = low.astype(BF)
    pad_ref[1, at, :, lanes] = row.astype(BF)
    pad_ref[2, at, :, lanes] = high.astype(BF)


def place_columns(got_left, got_right, left_ref, right_ref):
    rows = got_left.shape[0] - 32
    left_ref[...] = got_left.astype(F32)
    right_ref[...] = got_right.astype(F32)
    for at in (rows, rows + 16):
        left_ref[at : at + 1, :] = left_ref[at + 15 : at + 16, :]


def put_pairs(x_ref, start, count, left_ref, right_ref, pad_ref):
    for k in range(count):
        m = start + k
        put_row(x_ref[2 * m], 2 * m, m, 1, left_ref, right_ref, pad_ref)
        put_row(x_ref[2 * m + 1], 2 * m + 1, m + 1, 0, left_ref, right_ref, pad_ref)


def windows(pad_ref, start, count):
    cells, lanes = pad_ref.shape[2:]
    return jnp.concatenate(
        [
            pad_ref[d, pl.ds(start + h, count)].reshape(count * cells, lanes)
            for h in range(2)
            for d in range(3)
        ],
        axis=1,
    )


def lane_of(rho, d):
    return ((rho // 2) * 3 + d) * 2 + rho % 2


def start_all(copies):
    for copy in copies:
        copy.start()


def wait_all(copies):
    for copy in copies:
        copy.wait()


def pack_kernel(
    coarse_ref, small_ref, cot_hbm, own_ref, all_ref, down_ref, up_ref,
    work_ref, meta_ref, sems,
):
    per, variables, chans = coarse_ref.shape
    rows, cells = cot_hbm.shape[:2]
    copies = [
        pltpu.make_async_copy(cot_hbm.at[rows - 1], down_ref.at[pl.ds(META, cells)], sems.at[0]),
        pltpu.make_async_copy(cot_hbm.at[0], up_ref.at[pl.ds(META, cells)], sems.at[1]),
    ]
    start_all(copies)
    work_ref[...] = jnp.zeros_like(work_ref)
    for n in range(per):
        work_ref[n * VP : n * VP + variables, :] = coarse_ref[n].astype(F32)
    work = work_ref[...].astype(BF)
    own_ref[...] = work
    for target in range(all_ref.shape[0]):
        all_ref[target] = work
    meta_ref[...] = jnp.zeros_like(meta_ref)
    slots = small_ref.shape[1] // 2
    meta_ref[0:1, :slots] = small_ref[:, :slots].astype(F32)
    meta_ref[1:2, :slots] = small_ref[:, slots:].astype(F32)
    down_ref[:META, :] = meta_ref[...].astype(BF)
    up_ref[:META, :] = meta_ref[...].astype(BF)
    wait_all(copies)


def fill_columns(got_left, got_right, above_ref, below_ref, left_ref, right_ref, pad_ref):
    cells = pad_ref.shape[2]
    rows = got_left.shape[0] - 32
    place_columns(got_left, got_right, left_ref, right_ref)
    base = above_ref.shape[0] - cells
    put_row(above_ref[base:, :], rows + 16, 0, 0, left_ref, right_ref, pad_ref)
    put_row(below_ref[base:, :], rows, rows // 2, 1, left_ref, right_ref, pad_ref)


def back_kernel(
    cot_hbm, above_ref, below_ref, left16_ref, right16_ref, w_ref,
    back_hbm, cot_ref, back_ref, pad_ref, taps_ref, left_ref, right_ref, in_sems, out_sems,
):
    pairs, _, cells, chans = back_ref.shape
    count = PAIRS
    groups = pairs // count

    def fetch(g):
        at = pl.ds(g * 2 * count, 2 * count)
        return pltpu.make_async_copy(cot_hbm.at[at], cot_ref.at[at], in_sems.at[g])

    def send(g):
        at = pl.ds(g * count, count)
        return pltpu.make_async_copy(back_ref.at[at], back_hbm.at[at], out_sems.at[g])

    start_all([fetch(g) for g in range(groups)])
    taps_ref[...] = jnp.zeros_like(taps_ref)
    for dy in range(3):
        for dx in range(3):
            for o in range(2):
                col = lane_of(o + 2 - dy, 2 - dx) * chans
                taps_ref[o * chans : (o + 1) * chans, col : col + chans] = w_ref[3 * dy + dx]
    fill_columns(
        left16_ref[...], right16_ref[...], above_ref, below_ref, left_ref, right_ref, pad_ref
    )

    def pad(g, _):
        fetch(g).wait()
        put_pairs(cot_ref, g * count, count, left_ref, right_ref, pad_ref)
        return 0

    lax.fori_loop(0, groups, pad, 0)

    def step(g, _):
        acc = mm_t(windows(pad_ref, g * count, count), taps_ref[...]).astype(BF)
        for o in range(2):
            part = acc[:, o * chans : (o + 1) * chans].reshape(count, cells, chans)
            back_ref[pl.ds(g * count, count), o] = part
        send(g).start()
        return 0

    lax.fori_loop(0, groups, step, 0)
    wait_all([send(g) for g in range(groups)])


def conv_kernel(
    pos_ref, smooth_hbm, above_ref, below_ref, got_left_ref, got_right_ref, w_ref, act_hbm,
    out_hbm, smooth_ref, act_ref, out_ref, pad_ref, taps_ref, left_ref, right_ref, sems,
):
    pairs, _, cells, chans = out_ref.shape
    rows = 2 * pairs
    count = PAIRS
    groups = pairs // count

    def piece(src, dst, kind, g, size):
        at = pl.ds(g * size, size)
        return pltpu.make_async_copy(src.at[at], dst.at[at], sems.at[kind, g])

    def fetch(g):
        return piece(smooth_hbm, smooth_ref, 0, g, 2 * count)

    def fetch_act(g):
        return piece(act_hbm, act_ref, 1, g, count)

    def send(g):
        return piece(out_ref, out_hbm, 2, g, count)

    start_all([fetch(g) for g in range(groups)])
    start_all([fetch_act(g) for g in range(groups)])
    taps_ref[...] = jnp.zeros_like(taps_ref)
    for dy in range(3):
        for dx in range(3):
            for o in range(2):
                row = lane_of(o + dy, dx) * chans
                taps_ref[row : row + chans, o * chans : (o + 1) * chans] = w_ref[3 * dy + dx]
    gx, n_gx = pos_ref[1], pos_ref[2]
    base = got_left_ref.shape[0] - rows - 32
    from_left = jnp.where(gx > 0, got_left_ref[base:, :].astype(F32), 0.0)
    from_right = jnp.where(gx < n_gx - 1, got_right_ref[base:, :].astype(F32), 0.0)
    fill_columns(from_left, from_right, above_ref, below_ref, left_ref, right_ref, pad_ref)

    def pad(g, _):
        fetch(g).wait()
        put_pairs(smooth_ref, g * count, count, left_ref, right_ref, pad_ref)
        return 0

    lax.fori_loop(0, groups, pad, 0)

    def step(g, _):
        fetch_act(g).wait()
        acc = mm(windows(pad_ref, g * count, count), taps_ref[...])
        for o in range(2):
            part = acc[:, o * chans : (o + 1) * chans].reshape(count, cells, chans)
            act = act_ref[pl.ds(g * count, count), o].astype(F32)
            out_ref[pl.ds(g * count, count), o] = (act + part).astype(BF)
        send(g).start()
        return 0

    lax.fori_loop(0, groups, step, 0)
    wait_all([send(g) for g in range(groups)])


def main_kernel(
    pos_ref, ids_ref, which_ref, noise_index_ref, noise_ref, band_above_ref, band_own_ref, band_below_ref, weight_ref,
    bias_col_ref, above_ref, below_ref, left16_ref, right16_ref,
    fine_hbm, cot_hbm, back_hbm, table_hbm,
    smooth_hbm, act_hbm, gfine_hbm, edges_ref, terms_ref, down_ref, up_ref, shared_ref,
    pad_ref, cot_ref, fine_ref, back_ref, table_ref, smooth_ref, act_ref, gfine_ref,
    coarse_ref, slope_ref, gpre_ref, enc_ref, enc16_ref, terms_acc, flip_ref,
    left_ref, right_ref, in_sems, out_sems,
):
    total_rows, cells, chans = fine_ref.shape
    slots = which_ref.shape[1]
    mats = table_ref.shape[0]
    rows = CHUNK
    steps = total_rows // rows
    pairs = total_rows // 2
    rowblk = band_own_ref.shape[0] // VP
    first_band = pos_ref[0] * rowblk - rowblk

    def fetches(step):
        at = pl.ds(step * rows, rows)
        flat = pl.ds(step * rows * cells, rows * cells)
        return [
            pltpu.make_async_copy(table_hbm.at[:, flat], table_ref.at[:, flat], in_sems.at[0, step]),
            pltpu.make_async_copy(fine_hbm.at[at], fine_ref.at[at], in_sems.at[1, step]),
            pltpu.make_async_copy(back_hbm.at[at], back_ref.at[at], in_sems.at[2, step]),
            pltpu.make_async_copy(cot_hbm.at[at], cot_ref.at[at], in_sems.at[3, step]),
        ]

    def sends(step):
        at = pl.ds(step * rows, rows)
        return [
            pltpu.make_async_copy(smooth_ref.at[at], smooth_hbm.at[at], out_sems.at[0, step]),
            pltpu.make_async_copy(act_ref.at[at], act_hbm.at[at], out_sems.at[1, step]),
            pltpu.make_async_copy(gfine_ref.at[at], gfine_hbm.at[at], out_sems.at[2, step]),
        ]

    for step in range(steps):
        start_all(fetches(step))
    enc_ref[...] = jnp.zeros_like(enc_ref)
    terms_acc[...] = jnp.zeros_like(terms_acc)
    group = 4

    def encode(first, _):
        for k in range(group):
            slot = first * group + k
            at = ids_ref[0, slot] - first_band
            band = lax.div(at, rowblk)
            source = pl.ds(pl.multiple_of(lax.rem(at, rowblk) * VP, VP), VP)
            block = jnp.where(
                band == 1,
                band_own_ref[source, :],
                jnp.where(band == 0, band_above_ref[source, :], band_below_ref[source, :]),
            )
            coarse_ref[:, pl.ds(pl.multiple_of(slot * cells, cells), cells)] = block
        size = group * cells
        lanes = pl.ds(pl.multiple_of(first * size, size), size)
        pre = t_mm(weight_ref[...], coarse_ref[:, lanes]) + bias_col_ref[...]
        sig = sigmoid(pre)
        encoded = (pre * sig).astype(BF).astype(F32)
        slope_ref[:, lanes] = sig * (1.0 + pre * (1.0 - sig))
        for k in range(group):
            enc_ref[which_ref[0, first * group + k]] += encoded[:, k * cells : (k + 1) * cells]
        return 0

    lax.fori_loop(0, slots // group, encode, 0)
    for w in range(mats):
        enc16_ref[:, w * cells : (w + 1) * cells] = enc_ref[w].astype(BF)
    embed = noise_ref[pl.ds(noise_index_ref[0], 1), :]
    fill_columns(
        left16_ref[...], right16_ref[...], above_ref, below_ref, left_ref, right_ref, pad_ref
    )

    def chunk(step, _):
        wait_all(fetches(step))
        at = pl.ds(step * rows, rows)
        flat = pl.ds(pl.multiple_of(step * rows * cells, rows * cells), rows * cells)
        table = jnp.concatenate([table_ref[w, flat, :] for w in range(mats)], axis=1)
        lifted = mm_t(table, enc16_ref[...])
        fine = fine_ref[at].reshape(rows * cells, chans).astype(F32)
        act = fine + lifted + embed
        sig = sigmoid(act)
        smooth = act * sig
        slope = sig * (1.0 + act * (1.0 - sig))
        cot = cot_ref[at].reshape(rows * cells, chans).astype(F32)
        back = back_ref[at].reshape(rows * cells, chans).astype(F32)
        gfine = (cot + slope * back).astype(BF)
        act_ref[at] = act.astype(BF).reshape(rows, cells, chans)
        gfine_ref[at] = gfine.reshape(rows, cells, chans)
        smooth3 = smooth.reshape(rows, cells, chans)
        smooth16 = smooth3.astype(BF)
        smooth_ref[at] = smooth16
        for r in range(rows):
            row = pl.ds(step * rows + r, 1)
            edges_ref[0, row, :] = smooth3[r, 0:1, :]
            edges_ref[1, row, :] = smooth3[r, cells - 1 : cells, :]
            lanes = pl.ds(pl.multiple_of((step * (rows // 2) + r // 2) * cells, cells), cells)
            flip_ref[(r % 2) * chans : (r % 2 + 1) * chans, lanes] = smooth16[r].T
        put_pairs(cot_ref, step * (rows // 2), rows // 2, left_ref, right_ref, pad_ref)
        terms_acc[...] += mm(gfine.T, table)
        return 0

    lax.fori_loop(0, steps, chunk, 0)
    for step in range(steps):
        start_all(sends(step))

    size = mats * chans
    for w in range(mats):
        terms = terms_acc[:, w * cells : (w + 1) * cells]
        terms_ref[w] = terms
        down_ref[w * chans : (w + 1) * chans, :] = terms.astype(BF)
        up_ref[w * chans : (w + 1) * chans, :] = terms.astype(BF)
    down_ref[size:, :] = smooth_ref[total_rows - 1]
    up_ref[size:, :] = smooth_ref[0]

    def conv_grad(d):
        found = []
        for h in range(2):
            rhs = pad_ref[d, h : h + pairs].reshape(pairs * cells, 2 * chans)
            found.append(mm(flip_ref[...], rhs))
        for dy in range(3):
            total = jnp.zeros((chans, chans), F32)
            for o in range(2):
                rho = o + 2 - dy
                lanes = slice(rho % 2 * chans, (rho % 2 + 1) * chans)
                total = total + found[rho // 2][o * chans : (o + 1) * chans, lanes]
            tap = (3 * dy + 2 - d) * chans
            shared_ref[pl.ds(tap, chans), :] = total.astype(BF)

    for d in range(3):
        conv_grad(d)

    def slot_grad(slot, gsum):
        lanes = pl.ds(pl.multiple_of(slot * cells, cells), cells)
        gpre = terms_ref[which_ref[0, slot]] * slope_ref[:, lanes]
        gpre_ref[:, lanes] = gpre.astype(BF)
        return gsum + gpre

    gsum = lax.fori_loop(0, slots, slot_grad, jnp.zeros((chans, cells), F32), unroll=2)
    gweight = mm_t(coarse_ref[...], gpre_ref[...])
    ones = jnp.ones((16, cells), BF)
    high = gsum.astype(BF)
    gbias = mm_t(ones, high) + mm_t(ones, (gsum - high.astype(F32)).astype(BF))
    base = 9 * chans
    for part in (gweight, gbias):
        count = part.shape[0]
        high = part.astype(BF)
        shared_ref[base : base + count, :] = high
        shared_ref[base + count : base + 2 * count, :] = (part - high.astype(F32)).astype(BF)
        base += 2 * count
    shared_ref[base:, :] = jnp.zeros((shared_ref.shape[0] - base, chans), BF)
    for step in range(steps):
        wait_all(sends(step))


def band_kernel(
    pos_ref, loc_ref, which_ref, above_ref, own_ref, below_ref, edges_ref,
    mine_ref, *refs,
):
    outs, acc_ref = refs[:-1], refs[-1]
    acc_ref[...] = jnp.zeros_like(acc_ref)
    rowblk, chans, cells = acc_ref.shape

    def slot_terms(slot, _):
        for tile in range(3):
            at, w = loc_ref[tile, slot], which_ref[tile, slot]

            @pl.when(jnp.logical_and(at >= 0, at < rowblk))
            def _():
                if tile == 1:
                    acc_ref[at] += own_ref[w]
                else:
                    terms = (above_ref, below_ref)[tile // 2]
                    rows = pl.ds(pl.multiple_of(w * chans, chans), chans)
                    acc_ref[at] += terms[rows, :].astype(F32)

        return 0

    lax.fori_loop(0, which_ref.shape[1], slot_terms, 0)
    gx, n_gx = pos_ref[1], len(outs) + 1
    per = rowblk // n_gx
    for n in range(per):
        mine_ref[n] = acc_ref[gx * per + n]
    for k, out_ref in enumerate(outs, 1):
        target = lax.rem(gx + k, n_gx)
        for n in range(per):
            out_ref[n * chans : (n + 1) * chans, :] = acc_ref[target * per + n].astype(BF)
    if not outs:
        return
    size = above_ref.shape[0] - cells
    base = per * chans
    edge = edges_ref.shape[1]
    for out_ref, column, first in ((outs[0], 1, cells - 16), (outs[-1], 0, 0)):
        rows = slice(first, first + 16)
        out_ref[base : base + edge, :] = edges_ref[column].astype(BF)
        out_ref[base + edge : base + edge + 16, :] = below_ref[size:, :][rows]
        out_ref[base + edge + 16 :, :] = above_ref[size:, :][rows]


def owner_kernel(mine_ref, coarse_ref, weight_ref, bias_col_ref, *refs):
    gots, out_ref = refs[:-1], refs[-1]
    weight = weight_ref[...]
    chans = weight.shape[1]
    for n in range(out_ref.shape[0]):
        total = mine_ref[n]
        for got_ref in gots:
            total = total + got_ref[n * chans : (n + 1) * chans, :].astype(F32)
        pre = t_mm(weight, coarse_ref[n * VP : (n + 1) * VP, :]) + bias_col_ref[...]
        sig = sigmoid(pre)
        gpre = total * (sig * (1.0 + pre * (1.0 - sig)))
        high = gpre.astype(BF)
        low = (gpre - high.astype(F32)).astype(BF)
        full = mm(weight, high) + mm(weight, low)
        out_ref[n] = full[: out_ref.shape[1], :]


def sum_kernel(got_ref, out_ref):
    total = jnp.sum(got_ref[...].astype(F32), axis=0).astype(BF)
    out_ref[...] = jnp.broadcast_to(total[None], out_ref.shape)


def finish_kernel(got_ref, gconv_ref, gweight_ref, gbias_ref):
    taps, chans, _ = gconv_ref.shape
    variables = gweight_ref.shape[0]
    for tap in range(taps):
        gconv_ref[tap] = got_ref[tap * chans : (tap + 1) * chans, :].astype(F32)
    base = taps * chans
    high = got_ref[base : base + VP, :].astype(F32)
    low = got_ref[base + VP : base + 2 * VP, :].astype(F32)
    gweight_ref[...] = (high + low)[:variables, :]
    base += 2 * VP
    high = got_ref[base : base + 16, :].astype(F32)
    low = got_ref[base + 16 : base + 32, :].astype(F32)
    gbias_ref[...] = (high + low)[:1, :]


def params(mib):
    return pltpu.CompilerParams(vmem_limit_bytes=mib * 1024 * 1024)


def shape(dims, dtype=BF):
    return jax.ShapeDtypeStruct(dims, dtype)


def cost(flops, size):
    return pl.CostEstimate(flops=flops, bytes_accessed=size, transcendentals=0)


def body(
    coarse,
    enc_weight,
    enc_bias,
    block_ids,
    interp_index,
    interp_table,
    noise_index,
    noise_table,
    fine,
    conv_weight,
    cotangent,
):
    n_gy, n_gx = lax.axis_size("gy"), lax.axis_size("gx")
    per, variables, chans = coarse.shape
    rows, cells, _ = fine.shape
    rowblk = per * n_gx
    slots = block_ids.shape[1]
    mats = interp_table.shape[0]
    pairs = rows // 2
    down = [(i, i + 1) for i in range(n_gy - 1)]
    up = [(i + 1, i) for i in range(n_gy - 1)]
    right = [(i, i + 1) for i in range(n_gx - 1)]
    left = [(i + 1, i) for i in range(n_gx - 1)]
    both = ("gy", "gx")
    gy = lax.axis_index("gy")
    pos = jnp.stack([gy, lax.axis_index("gx"), jnp.int32(n_gx)]).astype(jnp.int32)
    nown = per * VP

    own, spread, to_below, to_above = pl.pallas_call(
        pack_kernel,
        out_shape=(
            shape((nown, chans)),
            shape((n_gx, nown, chans)),
            shape((META + cells, chans)),
            shape((META + cells, chans)),
        ),
        in_specs=[VMEM, VMEM, HBM],
        out_specs=(VMEM,) * 4,
        scratch_shapes=[
            pltpu.VMEM((nown, chans), F32),
            pltpu.VMEM((META, chans), F32),
            pltpu.SemaphoreType.DMA((2,)),
        ],
        compiler_params=params(LIMIT),
        name="pack",
    )(coarse, jnp.concatenate([block_ids, interp_index], axis=1), cotangent)
    band_own = lax.all_to_all(spread, "gx", 0, 0, tiled=True).reshape(rowblk * VP, chans)
    from_above = lax.ppermute(to_below, "gy", down)
    from_below = lax.ppermute(to_above, "gy", up)
    to_left = jnp.concatenate(
        [cotangent[:, 0], from_below[META : META + 16], from_above[META : META + 16]]
    )
    to_right = jnp.concatenate(
        [
            cotangent[:, cells - 1],
            from_below[META + cells - 16 :],
            from_above[META + cells - 16 :],
        ]
    )
    cot_left = lax.ppermute(to_right, "gx", right)
    cot_right = lax.ppermute(to_left, "gx", left)
    band_above = lax.ppermute(band_own, "gy", down)
    band_below = lax.ppermute(band_own, "gy", up)

    weight_pad = jnp.pad(enc_weight, ((0, VP - variables), (0, 0)))
    bias_col = enc_bias.reshape(chans, 1)
    pad_shape = (3, pairs + 1, cells, 2 * chans)
    field = (rows, cells, chans)
    paired = (pairs, 2, cells, chans)
    columns = pltpu.VMEM((rows + 32, chans), F32)
    conv_flops = 2 * pairs * cells * 12 * chans * 2 * chans
    groups = pairs // PAIRS
    back = pl.pallas_call(
        back_kernel,
        out_shape=shape(paired),
        in_specs=[HBM] + [VMEM] * 5,
        out_specs=HBM,
        scratch_shapes=[
            pltpu.VMEM(field, BF),
            pltpu.VMEM(paired, BF),
            pltpu.VMEM(pad_shape, BF),
            pltpu.VMEM((2 * chans, 12 * chans), BF),
            columns,
            columns,
            pltpu.SemaphoreType.DMA((groups,)),
            pltpu.SemaphoreType.DMA((groups,)),
        ],
        compiler_params=params(LIMIT),
        cost_estimate=cost(conv_flops, 12 << 20),
        name="back",
    )(cotangent, from_above, from_below, cot_left, cot_right, conv_weight)

    n_dev = n_gy * n_gx
    steps = rows // CHUNK
    smooth, act, grad_fine, edges, terms, to_below, to_above, shared = pl.pallas_call(
        main_kernel,
        out_shape=(
            shape(field),
            shape(field),
            shape(field),
            shape((2, rows, chans), F32),
            shape((mats, chans, chans), F32),
            shape((mats * chans + cells, chans)),
            shape((mats * chans + cells, chans)),
            shape((n_dev * PACK, chans)),
        ),
        in_specs=[SMEM] * 4 + [VMEM] * 10 + [HBM] * 4,
        out_specs=(HBM,) * 3 + (VMEM,) * 5,
        scratch_shapes=[
            pltpu.VMEM(pad_shape, BF),
            pltpu.VMEM(field, BF),
            pltpu.VMEM(field, BF),
            pltpu.VMEM(field, BF),
            pltpu.VMEM(interp_table.shape, BF),
            pltpu.VMEM(field, BF),
            pltpu.VMEM(field, BF),
            pltpu.VMEM(field, BF),
            pltpu.VMEM((VP, slots * chans), BF),
            pltpu.VMEM((chans, slots * chans), F32),
            pltpu.VMEM((chans, slots * chans), BF),
            pltpu.VMEM((mats, chans, chans), F32),
            pltpu.VMEM((chans, mats * chans), BF),
            pltpu.VMEM((chans, mats * chans), F32),
            pltpu.VMEM((2 * chans, pairs * cells), BF),
            columns,
            columns,
            pltpu.SemaphoreType.DMA((4, steps)),
            pltpu.SemaphoreType.DMA((3, steps)),
        ],
        compiler_params=params(LIMIT),
        cost_estimate=cost(3 * conv_flops, 24 << 20),
        name="main",
    )(
        pos,
        block_ids,
        interp_index,
        noise_index,
        noise_table,
        band_above,
        band_own,
        band_below,
        weight_pad,
        bias_col,
        from_above,
        from_below,
        cot_left,
        cot_right,
        fine,
        cotangent,
        back.reshape(field),
        interp_table,
    )

    parts = lax.all_to_all(shared.reshape(n_dev, PACK, chans), both, 0, 0, tiled=True)

    below2 = lax.ppermute(to_above, "gy", up)
    above2 = lax.ppermute(to_below, "gy", down)
    above_meta = from_above[:2, :slots].astype(jnp.int32)
    below_meta = from_below[:2, :slots].astype(jnp.int32)
    loc_all = jnp.concatenate([above_meta[:1], block_ids, below_meta[:1]]) - gy * rowblk
    which_all = jnp.concatenate([above_meta[1:], interp_index, below_meta[1:]])
    plain, full = per * chans, per * chans + rows + 32
    lengths = [full if k in (1, n_gx - 1) else plain for k in range(1, n_gx)]
    mine, *sent = pl.pallas_call(
        band_kernel,
        out_shape=[shape((per, chans, chans), F32)] + [shape((n, chans)) for n in lengths],
        in_specs=[SMEM] * 3 + [VMEM] * 4,
        out_specs=[VMEM] * n_gx,
        scratch_shapes=[pltpu.VMEM((rowblk, chans, chans), F32)],
        compiler_params=params(8),
        cost_estimate=cost(1 << 22, 1 << 20),
        name="band",
    )(pos, loc_all, which_all, above2, terms, below2, edges)
    got = [
        lax.ppermute(part, "gx", [(i, (i + k) % n_gx) for i in range(n_gx)])
        for k, part in enumerate(sent, 1)
    ]

    summed = pl.pallas_call(
        sum_kernel,
        out_shape=shape((n_dev, PACK, chans)),
        in_specs=[VMEM],
        out_specs=VMEM,
        compiler_params=params(8),
        name="total",
    )(parts)
    total = lax.all_to_all(summed, both, 0, 0, tiled=True).reshape(n_dev * PACK, chans)

    output = pl.pallas_call(
        conv_kernel,
        out_shape=shape(paired),
        in_specs=[SMEM, HBM] + [VMEM] * 5 + [HBM],
        out_specs=HBM,
        scratch_shapes=[
            pltpu.VMEM(field, BF),
            pltpu.VMEM(paired, BF),
            pltpu.VMEM(paired, BF),
            pltpu.VMEM(pad_shape, BF),
            pltpu.VMEM((12 * chans, 2 * chans), BF),
            columns,
            columns,
            pltpu.SemaphoreType.DMA((3, groups)),
        ],
        compiler_params=params(LIMIT),
        cost_estimate=cost(conv_flops, 8 << 20),
        name="conv",
    )(pos, smooth, above2, below2, got[0], got[-1], conv_weight, act.reshape(paired))
    output, mine = lax.optimization_barrier((output, mine))
    grad_coarse = pl.pallas_call(
        owner_kernel,
        out_shape=shape(coarse.shape, F32),
        in_specs=[VMEM] * (3 + n_gx),
        out_specs=VMEM,
        compiler_params=params(8),
        name="owner",
    )(mine, own, weight_pad, bias_col, *got)
    grad_conv, grad_weight, grad_bias = pl.pallas_call(
        finish_kernel,
        out_shape=(
            shape((9, chans, chans), F32),
            shape((variables, chans), F32),
            shape((1, chans), F32),
        ),
        in_specs=[VMEM],
        out_specs=(VMEM,) * 3,
        compiler_params=params(8),
        name="finish",
    )(total)
    return (
        output.reshape(field),
        grad_fine,
        grad_coarse,
        grad_weight,
        grad_bias.reshape(chans),
        grad_conv,
    )


def solution(mesh):
    placed = (
        P(("gy", "gx"), None, None),
        P(),
        P(),
        P(("gy", "gx"), None),
        P(("gy", "gx"), None),
        P(),
        P(),
        P(),
        P("gy", "gx", None),
        P(),
        P("gy", "gx", None),
    )
    return jax.shard_map(
        body,
        mesh=mesh,
        in_specs=placed,
        out_specs=(
            P("gy", "gx", None),
            P("gy", "gx", None),
            P(("gy", "gx"), None, None),
            P(),
            P(),
            P(),
        ),
        check_vma=False,
    )
```

```python
import functools

import jax
import jax.numpy as jnp
from jax import lax
from jax.experimental import pallas as pl
from jax.experimental.pallas import tpu as pltpu
from jax.sharding import PartitionSpec as P

BF = jnp.bfloat16
F32 = jnp.float32
VP = 80
META = 16
CHUNK = 16
PAIRS = 8
PACK = 16
LIMIT = 52
VMEM = pl.BlockSpec(memory_space=pltpu.VMEM)
SMEM = pl.BlockSpec(memory_space=pltpu.SMEM)
HBM = pl.BlockSpec(memory_space=pl.ANY)


def mm(a, b):
    return jnp.dot(a, b, preferred_element_type=F32)


def mm_t(a, b):
    return lax.dot_general(a, b, (((1,), (1,)), ((), ())), preferred_element_type=F32)


def t_mm(a, b):
    return lax.dot_general(a, b, (((0,), (0,)), ((), ())), preferred_element_type=F32)


def sigmoid(v):
    return 0.5 * jnp.tanh(0.5 * v) + 0.5


def put_row(row, r, at, half, left_ref, right_ref, pad_ref):
    row = row.astype(F32)
    size, chans = row.shape
    cell = lax.broadcasted_iota(jnp.int32, row.shape, 0)
    low = jnp.where(cell == 0, left_ref[pl.ds(r, 1), :], pltpu.roll(row, 1, 0))
    high = jnp.where(cell == size - 1, right_ref[pl.ds(r, 1), :], pltpu.roll(row, size - 1, 0))
    lanes = slice(half * chans, (half + 1) * chans)
    pad_ref[0, at, :, lanes] = low.astype(BF)
    pad_ref[1, at, :, lanes] = row.astype(BF)
    pad_ref[2, at, :, lanes] = high.astype(BF)


def place_columns(got_left, got_right, left_ref, right_ref):
    rows = got_left.shape[0] - 32
    left_ref[...] = got_left.astype(F32)
    right_ref[...] = got_right.astype(F32)
    for at in (rows, rows + 16):
        left_ref[at : at + 1, :] = left_ref[at + 15 : at + 16, :]


def put_pairs(x_ref, start, count, left_ref, right_ref, pad_ref):
    for k in range(count):
        m = start + k
        put_row(x_ref[2 * m], 2 * m, m, 1, left_ref, right_ref, pad_ref)
        put_row(x_ref[2 * m + 1], 2 * m + 1, m + 1, 0, left_ref, right_ref, pad_ref)


def windows(pad_ref, start, count):
    cells, lanes = pad_ref.shape[2:]
    return jnp.concatenate(
        [
            pad_ref[d, pl.ds(start + h, count)].reshape(count * cells, lanes)
            for h in range(2)
            for d in range(3)
        ],
        axis=1,
    )


def lane_of(rho, d):
    return ((rho // 2) * 3 + d) * 2 + rho % 2


def start_all(copies):
    for copy in copies:
        copy.start()


def wait_all(copies):
    for copy in copies:
        copy.wait()


def pack_kernel(
    coarse_ref, small_ref, cot_hbm, own_ref, all_ref, down_ref, up_ref,
    work_ref, meta_ref, sems,
):
    per, variables, chans = coarse_ref.shape
    rows, cells = cot_hbm.shape[:2]
    copies = [
        pltpu.make_async_copy(cot_hbm.at[rows - 1], down_ref.at[pl.ds(META, cells)], sems.at[0]),
        pltpu.make_async_copy(cot_hbm.at[0], up_ref.at[pl.ds(META, cells)], sems.at[1]),
    ]
    start_all(copies)
    work_ref[...] = jnp.zeros_like(work_ref)
    for n in range(per):
        work_ref[n * VP : n * VP + variables, :] = coarse_ref[n].astype(F32)
    work = work_ref[...].astype(BF)
    own_ref[...] = work
    for target in range(all_ref.shape[0]):
        all_ref[target] = work
    meta_ref[...] = jnp.zeros_like(meta_ref)
    slots = small_ref.shape[1] // 2
    meta_ref[0:1, :slots] = small_ref[:, :slots].astype(F32)
    meta_ref[1:2, :slots] = small_ref[:, slots:].astype(F32)
    down_ref[:META, :] = meta_ref[...].astype(BF)
    up_ref[:META, :] = meta_ref[...].astype(BF)
    wait_all(copies)


def fill_columns(got_left, got_right, above_ref, below_ref, left_ref, right_ref, pad_ref):
    cells = pad_ref.shape[2]
    rows = got_left.shape[0] - 32
    place_columns(got_left, got_right, left_ref, right_ref)
    base = above_ref.shape[0] - cells
    put_row(above_ref[base:, :], rows + 16, 0, 0, left_ref, right_ref, pad_ref)
    put_row(below_ref[base:, :], rows, rows // 2, 1, left_ref, right_ref, pad_ref)


def back_kernel(
    cot_ref, above_ref, below_ref, left16_ref, right16_ref, w_ref,
    back_hbm, back_ref, pad_ref, taps_ref, left_ref, right_ref, out_sems,
):
    pairs, _, cells, chans = back_ref.shape
    count = PAIRS
    groups = pairs // count

    def send(g):
        at = pl.ds(g * count, count)
        return pltpu.make_async_copy(back_ref.at[at], back_hbm.at[at], out_sems.at[g])

    taps_ref[...] = jnp.zeros_like(taps_ref)
    for dy in range(3):
        for dx in range(3):
            for o in range(2):
                col = lane_of(o + 2 - dy, 2 - dx) * chans
                taps_ref[o * chans : (o + 1) * chans, col : col + chans] = w_ref[3 * dy + dx]
    fill_columns(
        left16_ref[...], right16_ref[...], above_ref, below_ref, left_ref, right_ref, pad_ref
    )

    def pad(g, _):
        put_pairs(cot_ref, g * count, count, left_ref, right_ref, pad_ref)
        return 0

    lax.fori_loop(0, groups, pad, 0)

    def step(g, _):
        acc = mm_t(windows(pad_ref, g * count, count), taps_ref[...]).astype(BF)
        for o in range(2):
            part = acc[:, o * chans : (o + 1) * chans].reshape(count, cells, chans)
            back_ref[pl.ds(g * count, count), o] = part
        send(g).start()
        return 0

    lax.fori_loop(0, groups, step, 0)
    wait_all([send(g) for g in range(groups)])


def conv_kernel(
    pos_ref, smooth_hbm, above_ref, below_ref, got_left_ref, got_right_ref, w_ref, act_hbm,
    out_hbm, smooth_ref, act_ref, out_ref, pad_ref, taps_ref, left_ref, right_ref, sems,
):
    pairs, _, cells, chans = out_ref.shape
    rows = 2 * pairs
    count = PAIRS
    groups = pairs // count

    def piece(src, dst, kind, g, size):
        at = pl.ds(g * size, size)
        return pltpu.make_async_copy(src.at[at], dst.at[at], sems.at[kind, g])

    def fetch(g):
        return piece(smooth_hbm, smooth_ref, 0, g, 2 * count)

    def fetch_act(g):
        return piece(act_hbm, act_ref, 1, g, count)

    def send(g):
        return piece(out_ref, out_hbm, 2, g, count)

    start_all([fetch(g) for g in range(groups)])
    start_all([fetch_act(g) for g in range(groups)])
    taps_ref[...] = jnp.zeros_like(taps_ref)
    for dy in range(3):
        for dx in range(3):
            for o in range(2):
                row = lane_of(o + dy, dx) * chans
                taps_ref[row : row + chans, o * chans : (o + 1) * chans] = w_ref[3 * dy + dx]
    gx, n_gx = pos_ref[1], pos_ref[2]
    base = got_left_ref.shape[0] - rows - 32
    from_left = jnp.where(gx > 0, got_left_ref[base:, :].astype(F32), 0.0)
    from_right = jnp.where(gx < n_gx - 1, got_right_ref[base:, :].astype(F32), 0.0)
    fill_columns(from_left, from_right, above_ref, below_ref, left_ref, right_ref, pad_ref)

    def pad(g, _):
        fetch(g).wait()
        put_pairs(smooth_ref, g * count, count, left_ref, right_ref, pad_ref)
        return 0

    lax.fori_loop(0, groups, pad, 0)

    def step(g, _):
        fetch_act(g).wait()
        acc = mm(windows(pad_ref, g * count, count), taps_ref[...])
        for o in range(2):
            part = acc[:, o * chans : (o + 1) * chans].reshape(count, cells, chans)
            act = act_ref[pl.ds(g * count, count), o].astype(F32)
            out_ref[pl.ds(g * count, count), o] = (act + part).astype(BF)
        send(g).start()
        return 0

    lax.fori_loop(0, groups, step, 0)
    wait_all([send(g) for g in range(groups)])


def main_kernel(
    pos_ref, ids_ref, which_ref, noise_index_ref, noise_ref, band_above_ref, band_own_ref, band_below_ref, weight_ref,
    bias_col_ref, above_ref, below_ref, left16_ref, right16_ref,
    fine_hbm, cot_hbm, back_hbm, table_hbm,
    smooth_hbm, act_hbm, gfine_hbm, edges_ref, terms_ref, down_ref, up_ref, shared_ref,
    pad_ref, cot_ref, fine_ref, back_ref, table_ref, smooth_ref, act_ref, gfine_ref,
    coarse_ref, slope_ref, gpre_ref, enc_ref, enc16_ref, terms_acc, flip_ref,
    left_ref, right_ref, in_sems, out_sems,
):
    total_rows, cells, chans = fine_ref.shape
    slots = which_ref.shape[1]
    mats = table_ref.shape[0]
    rows = CHUNK
    steps = total_rows // rows
    pairs = total_rows // 2
    rowblk = band_own_ref.shape[0] // VP
    first_band = pos_ref[0] * rowblk - rowblk

    def fetches(step):
        at = pl.ds(step * rows, rows)
        flat = pl.ds(step * rows * cells, rows * cells)
        return [
            pltpu.make_async_copy(table_hbm.at[:, flat], table_ref.at[:, flat], in_sems.at[0, step]),
            pltpu.make_async_copy(fine_hbm.at[at], fine_ref.at[at], in_sems.at[1, step]),
            pltpu.make_async_copy(back_hbm.at[at], back_ref.at[at], in_sems.at[2, step]),
            pltpu.make_async_copy(cot_hbm.at[at], cot_ref.at[at], in_sems.at[3, step]),
        ]

    def sends(step):
        at = pl.ds(step * rows, rows)
        return [
            pltpu.make_async_copy(smooth_ref.at[at], smooth_hbm.at[at], out_sems.at[0, step]),
            pltpu.make_async_copy(act_ref.at[at], act_hbm.at[at], out_sems.at[1, step]),
            pltpu.make_async_copy(gfine_ref.at[at], gfine_hbm.at[at], out_sems.at[2, step]),
        ]

    for step in range(steps):
        start_all(fetches(step))
    enc_ref[...] = jnp.zeros_like(enc_ref)
    terms_acc[...] = jnp.zeros_like(terms_acc)
    group = 4

    def encode(first, _):
        for k in range(group):
            slot = first * group + k
            at = ids_ref[0, slot] - first_band
            band = lax.div(at, rowblk)
            source = pl.ds(pl.multiple_of(lax.rem(at, rowblk) * VP, VP), VP)
            block = jnp.where(
                band == 1,
                band_own_ref[source, :],
                jnp.where(band == 0, band_above_ref[source, :], band_below_ref[source, :]),
            )
            coarse_ref[:, pl.ds(pl.multiple_of(slot * cells, cells), cells)] = block
        size = group * cells
        lanes = pl.ds(pl.multiple_of(first * size, size), size)
        pre = t_mm(weight_ref[...], coarse_ref[:, lanes]) + bias_col_ref[...]
        sig = sigmoid(pre)
        encoded = (pre * sig).astype(BF).astype(F32)
        slope_ref[:, lanes] = sig * (1.0 + pre * (1.0 - sig))
        for k in range(group):
            enc_ref[which_ref[0, first * group + k]] += encoded[:, k * cells : (k + 1) * cells]
        return 0

    lax.fori_loop(0, slots // group, encode, 0)
    for w in range(mats):
        enc16_ref[:, w * cells : (w + 1) * cells] = enc_ref[w].astype(BF)
    embed = noise_ref[pl.ds(noise_index_ref[0], 1), :]
    fill_columns(
        left16_ref[...], right16_ref[...], above_ref, below_ref, left_ref, right_ref, pad_ref
    )

    def chunk(step, _):
        wait_all(fetches(step))
        at = pl.ds(step * rows, rows)
        flat = pl.ds(pl.multiple_of(step * rows * cells, rows * cells), rows * cells)
        table = jnp.concatenate([table_ref[w, flat, :] for w in range(mats)], axis=1)
        lifted = mm_t(table, enc16_ref[...])
        fine = fine_ref[at].reshape(rows * cells, chans).astype(F32)
        act = fine + lifted + embed
        sig = sigmoid(act)
        smooth = act * sig
        slope = sig * (1.0 + act * (1.0 - sig))
        cot = cot_ref[at].reshape(rows * cells, chans).astype(F32)
        back = back_ref[at].reshape(rows * cells, chans).astype(F32)
        gfine = (cot + slope * back).astype(BF)
        act_ref[at] = act.astype(BF).reshape(rows, cells, chans)
        gfine_ref[at] = gfine.reshape(rows, cells, chans)
        smooth3 = smooth.reshape(rows, cells, chans)
        smooth16 = smooth3.astype(BF)
        smooth_ref[at] = smooth16
        for r in range(rows):
            row = pl.ds(step * rows + r, 1)
            edges_ref[0, row, :] = smooth3[r, 0:1, :]
            edges_ref[1, row, :] = smooth3[r, cells - 1 : cells, :]
            lanes = pl.ds(pl.multiple_of((step * (rows // 2) + r // 2) * cells, cells), cells)
            flip_ref[(r % 2) * chans : (r % 2 + 1) * chans, lanes] = smooth16[r].T
        put_pairs(cot_ref, step * (rows // 2), rows // 2, left_ref, right_ref, pad_ref)
        terms_acc[...] += mm(gfine.T, table)
        return 0

    lax.fori_loop(0, steps, chunk, 0)
    for step in range(steps):
        start_all(sends(step))

    size = mats * chans
    for w in range(mats):
        terms = terms_acc[:, w * cells : (w + 1) * cells]
        terms_ref[w] = terms
        down_ref[w * chans : (w + 1) * chans, :] = terms.astype(BF)
        up_ref[w * chans : (w + 1) * chans, :] = terms.astype(BF)
    down_ref[size:, :] = smooth_ref[total_rows - 1]
    up_ref[size:, :] = smooth_ref[0]

    def conv_grad(d):
        found = []
        for h in range(2):
            rhs = pad_ref[d, h : h + pairs].reshape(pairs * cells, 2 * chans)
            found.append(mm(flip_ref[...], rhs))
        for dy in range(3):
            total = jnp.zeros((chans, chans), F32)
            for o in range(2):
                rho = o + 2 - dy
                lanes = slice(rho % 2 * chans, (rho % 2 + 1) * chans)
                total = total + found[rho // 2][o * chans : (o + 1) * chans, lanes]
            tap = (3 * dy + 2 - d) * chans
            shared_ref[pl.ds(tap, chans), :] = total.astype(BF)

    for d in range(3):
        conv_grad(d)

    def slot_grad(slot, gsum):
        lanes = pl.ds(pl.multiple_of(slot * cells, cells), cells)
        gpre = terms_ref[which_ref[0, slot]] * slope_ref[:, lanes]
        gpre_ref[:, lanes] = gpre.astype(BF)
        return gsum + gpre

    gsum = lax.fori_loop(0, slots, slot_grad, jnp.zeros((chans, cells), F32), unroll=2)
    gweight = mm_t(coarse_ref[...], gpre_ref[...])
    ones = jnp.ones((16, cells), BF)
    high = gsum.astype(BF)
    gbias = mm_t(ones, high) + mm_t(ones, (gsum - high.astype(F32)).astype(BF))
    base = 9 * chans
    for part in (gweight, gbias):
        count = part.shape[0]
        high = part.astype(BF)
        shared_ref[base : base + count, :] = high
        shared_ref[base + count : base + 2 * count, :] = (part - high.astype(F32)).astype(BF)
        base += 2 * count
    shared_ref[base:, :] = jnp.zeros((shared_ref.shape[0] - base, chans), BF)
    for step in range(steps):
        wait_all(sends(step))


def band_kernel(
    pos_ref, loc_ref, which_ref, above_ref, own_ref, below_ref, edges_ref,
    mine_ref, *refs,
):
    outs, acc_ref = refs[:-1], refs[-1]
    acc_ref[...] = jnp.zeros_like(acc_ref)
    rowblk, chans, cells = acc_ref.shape

    def slot_terms(slot, _):
        for tile in range(3):
            at, w = loc_ref[tile, slot], which_ref[tile, slot]

            @pl.when(jnp.logical_and(at >= 0, at < rowblk))
            def _():
                if tile == 1:
                    acc_ref[at] += own_ref[w]
                else:
                    terms = (above_ref, below_ref)[tile // 2]
                    rows = pl.ds(pl.multiple_of(w * chans, chans), chans)
                    acc_ref[at] += terms[rows, :].astype(F32)

        return 0

    lax.fori_loop(0, which_ref.shape[1], slot_terms, 0)
    gx, n_gx = pos_ref[1], len(outs) + 1
    per = rowblk // n_gx
    for n in range(per):
        mine_ref[n] = acc_ref[gx * per + n]
    for k, out_ref in enumerate(outs, 1):
        target = lax.rem(gx + k, n_gx)
        for n in range(per):
            out_ref[n * chans : (n + 1) * chans, :] = acc_ref[target * per + n].astype(BF)
    if not outs:
        return
    size = above_ref.shape[0] - cells
    base = per * chans
    edge = edges_ref.shape[1]
    for out_ref, column, first in ((outs[0], 1, cells - 16), (outs[-1], 0, 0)):
        rows = slice(first, first + 16)
        out_ref[base : base + edge, :] = edges_ref[column].astype(BF)
        out_ref[base + edge : base + edge + 16, :] = below_ref[size:, :][rows]
        out_ref[base + edge + 16 :, :] = above_ref[size:, :][rows]


def owner_kernel(mine_ref, coarse_ref, weight_ref, bias_col_ref, *refs):
    gots, out_ref = refs[:-1], refs[-1]
    weight = weight_ref[...]
    chans = weight.shape[1]
    for n in range(out_ref.shape[0]):
        total = mine_ref[n]
        for got_ref in gots:
            total = total + got_ref[n * chans : (n + 1) * chans, :].astype(F32)
        pre = t_mm(weight, coarse_ref[n * VP : (n + 1) * VP, :]) + bias_col_ref[...]
        sig = sigmoid(pre)
        gpre = total * (sig * (1.0 + pre * (1.0 - sig)))
        high = gpre.astype(BF)
        low = (gpre - high.astype(F32)).astype(BF)
        full = mm(weight, high) + mm(weight, low)
        out_ref[n] = full[: out_ref.shape[1], :]


def sum_kernel(got_ref, out_ref):
    total = jnp.sum(got_ref[...].astype(F32), axis=0).astype(BF)
    out_ref[...] = jnp.broadcast_to(total[None], out_ref.shape)


def finish_kernel(got_ref, gconv_ref, gweight_ref, gbias_ref):
    taps, chans, _ = gconv_ref.shape
    variables = gweight_ref.shape[0]
    for tap in range(taps):
        gconv_ref[tap] = got_ref[tap * chans : (tap + 1) * chans, :].astype(F32)
    base = taps * chans
    high = got_ref[base : base + VP, :].astype(F32)
    low = got_ref[base + VP : base + 2 * VP, :].astype(F32)
    gweight_ref[...] = (high + low)[:variables, :]
    base += 2 * VP
    high = got_ref[base : base + 16, :].astype(F32)
    low = got_ref[base + 16 : base + 32, :].astype(F32)
    gbias_ref[...] = (high + low)[:1, :]


def params(mib):
    return pltpu.CompilerParams(vmem_limit_bytes=mib * 1024 * 1024)


def shape(dims, dtype=BF):
    return jax.ShapeDtypeStruct(dims, dtype)


def cost(flops, size):
    return pl.CostEstimate(flops=flops, bytes_accessed=size, transcendentals=0)


def body(
    coarse,
    enc_weight,
    enc_bias,
    block_ids,
    interp_index,
    interp_table,
    noise_index,
    noise_table,
    fine,
    conv_weight,
    cotangent,
):
    n_gy, n_gx = lax.axis_size("gy"), lax.axis_size("gx")
    per, variables, chans = coarse.shape
    rows, cells, _ = fine.shape
    rowblk = per * n_gx
    slots = block_ids.shape[1]
    mats = interp_table.shape[0]
    pairs = rows // 2
    down = [(i, i + 1) for i in range(n_gy - 1)]
    up = [(i + 1, i) for i in range(n_gy - 1)]
    right = [(i, i + 1) for i in range(n_gx - 1)]
    left = [(i + 1, i) for i in range(n_gx - 1)]
    both = ("gy", "gx")
    gy = lax.axis_index("gy")
    pos = jnp.stack([gy, lax.axis_index("gx"), jnp.int32(n_gx)]).astype(jnp.int32)
    nown = per * VP

    own, spread, to_below, to_above = pl.pallas_call(
        pack_kernel,
        out_shape=(
            shape((nown, chans)),
            shape((n_gx, nown, chans)),
            shape((META + cells, chans)),
            shape((META + cells, chans)),
        ),
        in_specs=[VMEM, VMEM, HBM],
        out_specs=(VMEM,) * 4,
        scratch_shapes=[
            pltpu.VMEM((nown, chans), F32),
            pltpu.VMEM((META, chans), F32),
            pltpu.SemaphoreType.DMA((2,)),
        ],
        compiler_params=params(LIMIT),
        name="pack",
    )(coarse, jnp.concatenate([block_ids, interp_index], axis=1), cotangent)
    band_own = lax.all_to_all(spread, "gx", 0, 0, tiled=True).reshape(rowblk * VP, chans)
    from_above = lax.ppermute(to_below, "gy", down)
    from_below = lax.ppermute(to_above, "gy", up)
    to_left = jnp.concatenate(
        [cotangent[:, 0], from_below[META : META + 16], from_above[META : META + 16]]
    )
    to_right = jnp.concatenate(
        [
            cotangent[:, cells - 1],
            from_below[META + cells - 16 :],
            from_above[META + cells - 16 :],
        ]
    )
    cot_left = lax.ppermute(to_right, "gx", right)
    cot_right = lax.ppermute(to_left, "gx", left)
    band_above = lax.ppermute(band_own, "gy", down)
    band_below = lax.ppermute(band_own, "gy", up)

    weight_pad = jnp.pad(enc_weight, ((0, VP - variables), (0, 0)))
    bias_col = enc_bias.reshape(chans, 1)
    pad_shape = (3, pairs + 1, cells, 2 * chans)
    field = (rows, cells, chans)
    paired = (pairs, 2, cells, chans)
    columns = pltpu.VMEM((rows + 32, chans), F32)
    conv_flops = 2 * pairs * cells * 12 * chans * 2 * chans
    groups = pairs // PAIRS
    back = pl.pallas_call(
        back_kernel,
        out_shape=shape(paired),
        in_specs=[VMEM] * 6,
        out_specs=HBM,
        scratch_shapes=[
            pltpu.VMEM(paired, BF),
            pltpu.VMEM(pad_shape, BF),
            pltpu.VMEM((2 * chans, 12 * chans), BF),
            columns,
            columns,
            pltpu.SemaphoreType.DMA((groups,)),
        ],
        compiler_params=params(20),
        cost_estimate=cost(conv_flops, 12 << 20),
        name="back",
    )(cotangent, from_above, from_below, cot_left, cot_right, conv_weight)

    n_dev = n_gy * n_gx
    steps = rows // CHUNK
    smooth, act, grad_fine, edges, terms, to_below, to_above, shared = pl.pallas_call(
        main_kernel,
        out_shape=(
            shape(field),
            shape(field),
            shape(field),
            shape((2, rows, chans), F32),
            shape((mats, chans, chans), F32),
            shape((mats * chans + cells, chans)),
            shape((mats * chans + cells, chans)),
            shape((n_dev * PACK, chans)),
        ),
        in_specs=[SMEM] * 4 + [VMEM] * 10 + [HBM] * 4,
        out_specs=(HBM,) * 3 + (VMEM,) * 5,
        scratch_shapes=[
            pltpu.VMEM(pad_shape, BF),
            pltpu.VMEM(field, BF),
            pltpu.VMEM(field, BF),
            pltpu.VMEM(field, BF),
            pltpu.VMEM(interp_table.shape, BF),
            pltpu.VMEM(field, BF),
            pltpu.VMEM(field, BF),
            pltpu.VMEM(field, BF),
            pltpu.VMEM((VP, slots * chans), BF),
            pltpu.VMEM((chans, slots * chans), F32),
            pltpu.VMEM((chans, slots * chans), BF),
            pltpu.VMEM((mats, chans, chans), F32),
            pltpu.VMEM((chans, mats * chans), BF),
            pltpu.VMEM((chans, mats * chans), F32),
            pltpu.VMEM((2 * chans, pairs * cells), BF),
            columns,
            columns,
            pltpu.SemaphoreType.DMA((4, steps)),
            pltpu.SemaphoreType.DMA((3, steps)),
        ],
        compiler_params=params(LIMIT),
        cost_estimate=cost(3 * conv_flops, 24 << 20),
        name="main",
    )(
        pos,
        block_ids,
        interp_index,
        noise_index,
        noise_table,
        band_above,
        band_own,
        band_below,
        weight_pad,
        bias_col,
        from_above,
        from_below,
        cot_left,
        cot_right,
        fine,
        cotangent,
        back.reshape(field),
        interp_table,
    )

    parts = lax.all_to_all(shared.reshape(n_dev, PACK, chans), both, 0, 0, tiled=True)

    below2 = lax.ppermute(to_above, "gy", up)
    above2 = lax.ppermute(to_below, "gy", down)
    above_meta = from_above[:2, :slots].astype(jnp.int32)
    below_meta = from_below[:2, :slots].astype(jnp.int32)
    loc_all = jnp.concatenate([above_meta[:1], block_ids, below_meta[:1]]) - gy * rowblk
    which_all = jnp.concatenate([above_meta[1:], interp_index, below_meta[1:]])
    plain, full = per * chans, per * chans + rows + 32
    lengths = [full if k in (1, n_gx - 1) else plain for k in range(1, n_gx)]
    mine, *sent = pl.pallas_call(
        band_kernel,
        out_shape=[shape((per, chans, chans), F32)] + [shape((n, chans)) for n in lengths],
        in_specs=[SMEM] * 3 + [VMEM] * 4,
        out_specs=[VMEM] * n_gx,
        scratch_shapes=[pltpu.VMEM((rowblk, chans, chans), F32)],
        compiler_params=params(8),
        cost_estimate=cost(1 << 22, 1 << 20),
        name="band",
    )(pos, loc_all, which_all, above2, terms, below2, edges)
    got = [
        lax.ppermute(part, "gx", [(i, (i + k) % n_gx) for i in range(n_gx)])
        for k, part in enumerate(sent, 1)
    ]

    summed = pl.pallas_call(
        sum_kernel,
        out_shape=shape((n_dev, PACK, chans)),
        in_specs=[VMEM],
        out_specs=VMEM,
        compiler_params=params(8),
        name="total",
    )(parts)
    total = lax.all_to_all(summed, both, 0, 0, tiled=True).reshape(n_dev * PACK, chans)

    output = pl.pallas_call(
        conv_kernel,
        out_shape=shape(paired),
        in_specs=[SMEM, HBM] + [VMEM] * 5 + [HBM],
        out_specs=HBM,
        scratch_shapes=[
            pltpu.VMEM(field, BF),
            pltpu.VMEM(paired, BF),
            pltpu.VMEM(paired, BF),
            pltpu.VMEM(pad_shape, BF),
            pltpu.VMEM((12 * chans, 2 * chans), BF),
            columns,
            columns,
            pltpu.SemaphoreType.DMA((3, groups)),
        ],
        compiler_params=params(LIMIT),
        cost_estimate=cost(conv_flops, 8 << 20),
        name="conv",
    )(pos, smooth, above2, below2, got[0], got[-1], conv_weight, act.reshape(paired))
    output, mine = lax.optimization_barrier((output, mine))
    grad_coarse = pl.pallas_call(
        owner_kernel,
        out_shape=shape(coarse.shape, F32),
        in_specs=[VMEM] * (3 + n_gx),
        out_specs=VMEM,
        compiler_params=params(8),
        name="owner",
    )(mine, own, weight_pad, bias_col, *got)
    grad_conv, grad_weight, grad_bias = pl.pallas_call(
        finish_kernel,
        out_shape=(
            shape((9, chans, chans), F32),
            shape((variables, chans), F32),
            shape((1, chans), F32),
        ),
        in_specs=[VMEM],
        out_specs=(VMEM,) * 3,
        compiler_params=params(8),
        name="finish",
    )(total)
    return (
        output.reshape(field),
        grad_fine,
        grad_coarse,
        grad_weight,
        grad_bias.reshape(chans),
        grad_conv,
    )


def solution(mesh):
    placed = (
        P(("gy", "gx"), None, None),
        P(),
        P(),
        P(("gy", "gx"), None),
        P(("gy", "gx"), None),
        P(),
        P(),
        P(),
        P("gy", "gx", None),
        P(),
        P("gy", "gx", None),
    )
    return jax.shard_map(
        body,
        mesh=mesh,
        in_specs=placed,
        out_specs=(
            P("gy", "gx", None),
            P("gy", "gx", None),
            P(("gy", "gx"), None, None),
            P(),
            P(),
            P(),
        ),
        check_vma=False,
    )
```
